128 devices in a mesh: node: 8 (over x, core), local: 16 (over y, z).
Axes of the slice: x: 4, y: 4, z: 4, core: 2. Of those that a mesh axis runs over, the one named last changes fastest.
Arguments:
- tokens: bfloat16 [8192, 2048], P(('node', 'local')), may hold values from -6 to 6
- cotangent: bfloat16 [8192, 2048], P(('node', 'local')), may hold values from -6 to 6
- gate_weights: bfloat16 [8192, 6], P(('node', 'local')), may hold values from 0.099609375 to 1
- expert_ids: int32 [8192, 6], P(('node', 'local')), may hold values from 0 to 63, as said below
- gate_proj: bfloat16 [128, 2048, 704], P(('node', 'local')), may hold values from -0.125 to 0.125
- up_proj: bfloat16 [128, 2048, 704], P(('node', 'local')), may hold values from -0.125 to 0.125
- down_proj: bfloat16 [128, 704, 2048], P(('node', 'local')), may hold values from -0.15625 to 0.15625
Outputs:
- grad_tokens: bfloat16 [8192, 2048], P(('node', 'local'))
- grad_gates: float32 [8192, 6], P(('node', 'local'))
- grad_gate_proj: bfloat16 [128, 2048, 704], P(('node', 'local'))
- grad_up_proj: bfloat16 [128, 2048, 704], P(('node', 'local'))
- grad_down_proj: bfloat16 [128, 704, 2048], P(('node', 'local'))
The draws below stay inside these ranges and needn't reach their ends.
Inputs may be any that keep to these rules, and one draw needn't show every extreme that they name: `expert_ids`: each row names 6 different experts, two in each of three different groups of 8 consecutive experts. The 64 rows of one device name one expert at most 9 times, and on every device some expert is named exactly 9 times.
All inputs are finite; a program needn't handle non-finite values.
Results may differ from the reference program's by a relative error of at most 0.0057.
Values may be sent and summed in bfloat16 or wider, within the bound.
No kernel may reach another device: no remote copies, remote signals or barrier semaphores. Data moves between devices by JAX's collectives and lax.ppermute only.
A program may use at most 128 MiB of HBM per device.

```python
import jax
import jax.numpy as jnp
import numpy as np
from jax import lax

D = 2048
FF = 1408
EXPERTS = 64
TOP = 6
TOK_DEV = 64
SPLIT = 2
FFU = 704
UNITS = 128
TOKENS = 8192
CAP = 1152


def cell_table(doubled, removed):
    listing = []
    for first in range(8):
        for second in range(8):
            cell = (first, second)
            if cell in doubled:
                listing.extend([first * 8 + second, first * 8 + second])
            elif cell not in removed:
                listing.append(first * 8 + second)
    return np.array(listing, dtype=np.int32)


def draw_expert_ids(key, part):
    key = jax.random.fold_in(key, 7)
    key_shift, key_groups, key_members, key_table, key_perm, key_order = jax.random.split(key, 6)
    blocks = TOKENS // 64
    dev_count = TOKENS // TOK_DEV
    per_dev = TOK_DEV // 64
    table_one = jnp.asarray(cell_table(((0, 0), (5, 6), (3, 5)), ((1, 1), (2, 4), (6, 2))))
    table_two = jnp.asarray(cell_table(((0, 7), (5, 3), (3, 1)), ((4, 7), (7, 3), (2, 2))))
    picks = jax.random.randint(key_table, (blocks,), 0, 2)
    orders = jax.vmap(lambda sub: jax.random.permutation(sub, 64))(jax.random.split(key_perm, blocks))
    listing = jnp.where(picks[:, None] == 0, table_one[None, :], table_two[None, :])
    cells = jnp.take_along_axis(listing, orders, axis=1)
    shifts = jax.random.randint(key_shift, (dev_count, 2), 0, 8)
    block_shift = jnp.repeat(shifts, per_dev, axis=0)
    first = (cells // 8 + block_shift[:, 0:1]) % 8
    second = (cells % 8 + block_shift[:, 1:2]) % 8
    first = first.reshape(TOKENS)
    second = second.reshape(TOKENS)
    group_step = jnp.array([0, 0, 3, 3, 5, 5], dtype=jnp.int32)
    member_step = jnp.array([0, 1, 2, 5, 3, 7], dtype=jnp.int32)
    raw_group = (first[:, None] + group_step[None, :]) % 8
    raw_member = (second[:, None] + member_step[None, :]) % 8
    group_perm = jax.random.permutation(key_groups, 8)
    member_perm = jax.vmap(lambda sub: jax.random.permutation(sub, 8))(jax.random.split(key_members, 8))
    group = group_perm[raw_group]
    member = member_perm[group, raw_member]
    chosen = (group * 8 + member).astype(jnp.int32)
    scores = jax.random.randint(key_order, (TOKENS, 6), 0, 1 << 20) * 8 + jnp.arange(6, dtype=jnp.int32)[None, :]
    column_order = jnp.argsort(scores, axis=1, stable=True)
    return jnp.take_along_axis(chosen, column_order, axis=1).astype(jnp.int32)


def level_of(own_key, dims, cuts, low, high):
    factor_of = 1.0
    for axis_at, shards_of in cuts:
        draws = jax.random.uniform(jax.random.fold_in(jax.random.fold_in(own_key, 6), axis_at), (shards_of,), jnp.float32, low / len(cuts), high / len(cuts))
        factor_of = factor_of * jnp.repeat(jnp.exp(draws), dims[axis_at] // shards_of).reshape((-1,) + (1,) * (len(dims) - 1 - axis_at))
    return factor_of


def scatter_about(own_key, dims, deviation, most, cuts=(), kind=jnp.bfloat16):
    loudness = level_of(own_key, dims, cuts, -0.22, 0.18) if cuts else 1.0
    drawn = jax.random.normal(own_key, dims, jnp.float32) * deviation * loudness
    return jnp.minimum(jnp.maximum(drawn, -most), most).astype(kind)


def setup_inputs(seed: int = 0) -> dict:
    key_of = jax.random.split(jax.random.key(seed), 8)
    tokens = scatter_about(key_of[0], (TOKENS, D), 1.0, 6.0, ((0, 128),))
    cotangent = scatter_about(key_of[1], (TOKENS, D), 1.0, 6.0, ((0, 128),))
    gate_weights = jnp.clip(0.099609375 + 0.9003906 * jax.random.uniform(key_of[2], (TOKENS, TOP), jnp.float32) ** level_of(key_of[2], (TOKENS, TOP), ((0, 128),), -0.2, 0.2), 0.099609375, 1.0).astype(jnp.bfloat16)
    expert_ids = draw_expert_ids(jax.random.fold_in(key_of[7], 71), 0)
    gate_proj = scatter_about(key_of[4], (UNITS, D, FFU), D ** -0.5, 0.125, ((0, 128),))
    up_proj = scatter_about(key_of[5], (UNITS, D, FFU), D ** -0.5, 0.125, ((0, 128),))
    down_proj = scatter_about(key_of[6], (UNITS, FFU, D), FF ** -0.5, 0.15625, ((0, 128),))
    return dict(tokens=tokens, cotangent=cotangent, gate_weights=gate_weights, expert_ids=expert_ids, gate_proj=gate_proj, up_proj=up_proj, down_proj=down_proj)


def unit_pass(rows_x, rows_dy, rows_gate, gate_w, up_w, down_w):
    contract_cols = (((1,), (1,)), ((), ()))
    contract_rows = (((0,), (0,)), ((), ()))
    pre_gate = jnp.dot(rows_x, gate_w, preferred_element_type=jnp.float32)
    pre_up = jnp.dot(rows_x, up_w, preferred_element_type=jnp.float32)
    back_proj = lax.dot_general(rows_dy, down_w, contract_cols, preferred_element_type=jnp.float32)
    sigmoid_val = jax.nn.sigmoid(pre_gate)
    silu_val = pre_gate * sigmoid_val
    act = silu_val * pre_up
    gate_part = jnp.sum(act * back_proj, axis=1).astype(jnp.bfloat16)
    weight_col = rows_gate.astype(jnp.float32)[:, None]
    d_gate = (weight_col * back_proj * pre_up * sigmoid_val * (1.0 + pre_gate * (1.0 - sigmoid_val))).astype(jnp.bfloat16)
    d_up = (weight_col * back_proj * silu_val).astype(jnp.bfloat16)
    scaled = (weight_col * act).astype(jnp.bfloat16)
    token_term = (lax.dot_general(d_gate, gate_w, contract_cols, preferred_element_type=jnp.float32)
                  + lax.dot_general(d_up, up_w, contract_cols, preferred_element_type=jnp.float32)).astype(jnp.bfloat16)
    grad_gate = lax.dot_general(rows_x, d_gate, contract_rows, preferred_element_type=jnp.float32).astype(jnp.bfloat16)
    grad_up = lax.dot_general(rows_x, d_up, contract_rows, preferred_element_type=jnp.float32).astype(jnp.bfloat16)
    grad_down = lax.dot_general(scaled, rows_dy, contract_rows, preferred_element_type=jnp.float32).astype(jnp.bfloat16)
    return token_term, gate_part, grad_gate, grad_up, grad_down


def reference(tokens, cotangent, gate_weights, expert_ids, gate_proj, up_proj, down_proj):
    flat_ids = expert_ids.reshape(-1)
    assigned = TOKENS * TOP
    width = tokens.shape[1]
    padded_x = jnp.concatenate([tokens, jnp.zeros((1, width), tokens.dtype)], 0)
    padded_dy = jnp.concatenate([cotangent, jnp.zeros((1, width), cotangent.dtype)], 0)
    padded_gate = jnp.concatenate([gate_weights.reshape(-1), jnp.zeros((1,), gate_weights.dtype)], 0)
    gate_units = gate_proj.reshape(EXPERTS, SPLIT, width, FFU)
    up_units = up_proj.reshape(EXPERTS, SPLIT, width, FFU)
    down_units = down_proj.reshape(EXPERTS, SPLIT, FFU, width)

    def visit(carry, expert):
        grad_rows, grad_flat = carry
        picked = jnp.nonzero(flat_ids == expert, size=CAP, fill_value=assigned)[0].astype(jnp.int32)
        owners = (picked // TOP).astype(jnp.int32)
        rows_x = padded_x[owners]
        rows_dy = padded_dy[owners]
        rows_gate = padded_gate[picked]
        gate_list, up_list, down_list = [], [], []
        for half in range(SPLIT):
            token_term, gate_part, grad_gate, grad_up, grad_down = unit_pass(
                rows_x, rows_dy, rows_gate, gate_units[expert, half], up_units[expert, half], down_units[expert, half])
            grad_rows = grad_rows.at[owners].add(token_term.astype(jnp.float32))
            grad_flat = grad_flat.at[picked].add(gate_part.astype(jnp.float32))
            gate_list.append(grad_gate)
            up_list.append(grad_up)
            down_list.append(grad_down)
        return (grad_rows, grad_flat), (jnp.stack(gate_list, 0), jnp.stack(up_list, 0), jnp.stack(down_list, 0))

    start = (jnp.zeros((TOKENS + 1, width), jnp.float32), jnp.zeros((assigned + 1,), jnp.float32))
    (grad_rows, grad_flat), (grad_gate, grad_up, grad_down) = lax.scan(
        visit, start, jnp.arange(EXPERTS, dtype=jnp.int32))
    return (grad_rows[:TOKENS].astype(jnp.bfloat16),
            grad_flat[:assigned].reshape(TOKENS, TOP),
            grad_gate.reshape(UNITS, width, FFU),
            grad_up.reshape(UNITS, width, FFU),
            grad_down.reshape(UNITS, FFU, width))
```

```python
import jax
import jax.numpy as jnp
from jax import lax
from jax.experimental import pallas as pl
from jax.experimental.pallas import tpu as pltpu
from jax.sharding import PartitionSpec as P

LOW = 8
BF = jnp.bfloat16
F32 = jnp.float32
AXES = ("node", "local")
NT = (((1,), (1,)), ((), ()))
TN = (((0,), (0,)), ((), ()))


def dot(a, b, dims=(((1,), (0,)), ((), ()))):
    return lax.dot_general(a, b, dims, preferred_element_type=F32)


def column_tables(ids, first, columns, halves):
    tokens = ids.shape[0]
    col = lax.broadcasted_iota(jnp.int32, (tokens, columns), 1)
    expert = first + col // (halves * LOW)
    row = col % LOW
    hit = jnp.zeros((tokens, columns), F32)
    for k in range(ids.shape[1]):
        hit = hit + jnp.where(ids[:, k : k + 1] == expert, 1.0, 0.0)
    before = lax.broadcasted_iota(jnp.int32, (tokens, tokens), 1) < lax.broadcasted_iota(
        jnp.int32, (tokens, tokens), 0
    )
    rank = dot(jnp.where(before, 1.0, 0.0).astype(BF), hit.astype(BF)).astype(jnp.int32)
    return expert, row, hit, rank


def pack_kernel(halves, ids_ref, gates_ref, x_ref, dy_ref, out_ref):
    columns, width = out_ref.shape[0], x_ref.shape[1]
    ids = ids_ref[...]
    gates = gates_ref[...].astype(F32)
    first = pl.program_id(0) * (columns // (halves * LOW))
    expert, row, hit, rank = column_tables(ids, first, columns, halves)
    gate = jnp.zeros(hit.shape, F32)
    for k in range(ids.shape[1]):
        gate = gate + jnp.where(ids[:, k : k + 1] == expert, gates[:, k : k + 1], 0.0)
    low = jnp.where(rank == row, hit, 0.0)
    x, dy = x_ref[...], dy_ref[...]
    out_ref[:, :width] = dot(low.astype(BF), x, TN).astype(BF)
    out_ref[:, width : 2 * width] = dot((low * gate).astype(BF), dy, TN).astype(BF)
    last = jnp.where(rank == LOW, hit, 0.0)
    piece = 2 * width // LOW
    masks, pieces = [], []
    for i in range(LOW):
        at = i * piece
        source, weight = (x, last) if at < width else (dy, last * gate)
        masks.append(jnp.where(row == i, weight, 0.0).astype(BF))
        pieces.append(source[:, at % width : at % width + piece])
    out_ref[:, 2 * width :] = dot(
        jnp.concatenate(masks, 0), jnp.concatenate(pieces, 0), TN
    ).astype(BF)


def piece_table(sources):
    shape = (sources * LOW, sources * LOW)
    a = lax.broadcasted_iota(jnp.int32, shape, 0)
    b = lax.broadcasted_iota(jnp.int32, shape, 1)
    return jnp.where((a % sources) * LOW + a // sources == b, 1.0, 0.0).astype(BF)


def unit_kernel(
    got_ref, gate_ref, up_ref, down_ref,
    back_ref, dg_ref, du_ref, act_ref, dg9_ref, du9_ref, act9_ref, x9_ref, dy9_ref,
):
    rows, width = got_ref.shape[0], gate_ref.shape[1]
    sources = rows // LOW
    table = piece_table(sources)
    nine = dot(table, got_ref[:, 2 * width :]).astype(BF)
    nine = [nine[i * sources : (i + 1) * sources] for i in range(LOW)]
    x9 = jnp.concatenate(nine[: LOW // 2], 1)
    dy9 = jnp.concatenate(nine[LOW // 2 :], 1)
    x9_ref[...] = x9
    dy9_ref[...] = dy9
    x = jnp.concatenate([got_ref[:, :width], x9], 0)
    dy = jnp.concatenate([got_ref[:, width : 2 * width], dy9], 0)
    gate_w, up_w, down_w = gate_ref[...], up_ref[...], down_ref[...]
    pre_gate = dot(x, gate_w, NT)
    pre_up = dot(x, up_w, NT)
    back = dot(dy, down_w, NT)
    sig = jax.nn.sigmoid(pre_gate)
    silu = pre_gate * sig
    act = silu * pre_up
    part = jnp.sum(act * back, axis=1, keepdims=True)
    d_gate = (back * pre_up * sig * (1.0 + pre_gate * (1.0 - sig))).astype(BF)
    d_up = (back * silu).astype(BF)
    act = act.astype(BF)
    dg_ref[...], dg9_ref[...] = d_gate[:rows], d_gate[rows:]
    du_ref[...], du9_ref[...] = d_up[:rows], d_up[rows:]
    act_ref[...], act9_ref[...] = act[:rows], act[rows:]
    term = (dot(d_gate, gate_w) + dot(d_up, up_w)).astype(BF)
    back_ref[:, :width] = term[:rows]
    piece = width // LOW
    term9 = jnp.concatenate(
        [term[rows:, i * piece : (i + 1) * piece] for i in range(LOW)], 0
    )
    back_ref[:, width : width + piece] = dot(table, term9, TN).astype(BF)
    lane = lax.broadcasted_iota(jnp.int32, (rows, 128), 1)
    lane9 = lax.broadcasted_iota(jnp.int32, (sources, 128), 1)
    part9 = jnp.where(lane9 == 1, part[rows:], 0.0).astype(BF)
    parts = jnp.where(lane == 0, part[:rows], 0.0) + dot(table[:sources], part9, TN)
    back_ref[:, width + piece :] = parts.astype(BF)


def collect_kernel(halves, ids_ref, gates_ref, back_ref, out_ref, gg_ref, sum_ref, part_ref):
    columns, width = back_ref.shape[0], out_ref.shape[1]
    step = pl.program_id(0)
    ids = ids_ref[...]
    top = ids.shape[1]
    first = step * (columns // (halves * LOW))
    expert, row, hit, rank = column_tables(ids, first, columns, halves)
    low = jnp.where(rank == row, hit, 0.0)
    last = jnp.where(rank == LOW, hit, 0.0)

    @pl.when(step == 0)
    def _():
        sum_ref[...] = jnp.zeros_like(sum_ref)
        part_ref[...] = jnp.zeros_like(part_ref)

    piece = width // LOW
    sum_ref[...] += dot(low.astype(BF), back_ref[:, :width])
    pieces = back_ref[:, width : width + piece]
    for i in range(LOW):
        mask = jnp.where(row == i, last, 0.0).astype(BF)
        sum_ref[:, i * piece : (i + 1) * piece] += dot(mask, pieces)
    parts = back_ref[:, width + piece :]
    head = jnp.where(row == 0, last, 0.0)
    lane = lax.broadcasted_iota(jnp.int32, (ids.shape[0], 128), 1)
    for k in range(top):
        mine = ids[:, k : k + 1] == expert
        got = dot(jnp.where(mine, low, 0.0).astype(BF), parts)
        got9 = dot(jnp.where(mine, head, 0.0).astype(BF), parts)
        both = jnp.sum(
            jnp.where(lane == 0, got, 0.0) + jnp.where(lane == 1, got9, 0.0), axis=1, keepdims=True
        )
        part_ref[...] += jnp.where(lane == k, both, 0.0)

    @pl.when(step == pl.num_programs(0) - 1)
    def _():
        out_ref[...] = sum_ref[...].astype(BF)
        gg_ref[...] = part_ref[:, :top] / gates_ref[...].astype(F32)


def whole(shape):
    return pl.BlockSpec(shape, lambda b: (0,) * len(shape))


def split(shape):
    return pl.BlockSpec(shape, lambda b: (b,) + (0,) * (len(shape) - 1))


def limits(mib):
    return pltpu.CompilerParams(
        dimension_semantics=("arbitrary",), vmem_limit_bytes=mib * 2**20
    )


def local(tokens, cotangent, gate_weights, expert_ids, gate_proj, up_proj, down_proj):
    devices = lax.axis_size("node") * lax.axis_size("local")
    count, width = tokens.shape
    hidden = down_proj.shape[1]
    halves = 2
    experts = devices // halves
    slots = devices * LOW
    top = expert_ids.shape[1]

    blocks = 4
    message = 2 * width + 2 * width // LOW
    sent = pl.pallas_call(
        lambda *refs: pack_kernel(halves, *refs),
        grid=(blocks,),
        in_specs=[
            whole((count, top)), whole((count, top)), whole((count, width)), whole((count, width)),
        ],
        out_specs=split((slots // blocks, message)),
        out_shape=jax.ShapeDtypeStruct((slots, message), BF),
        compiler_params=limits(48),
        name="pack_rows",
    )(expert_ids, gate_weights, tokens, cotangent)

    got = lax.all_to_all(
        sent.reshape(devices, LOW, message), AXES, split_axis=0, concat_axis=0, tiled=True
    ).reshape(slots, message)

    gate_t = jnp.swapaxes(gate_proj[0], 0, 1)
    up_t = jnp.swapaxes(up_proj[0], 0, 1)
    down = down_proj[0]
    blocks = 4
    rows, rows9 = slots // blocks, devices // blocks
    reply = width + width // LOW + 128
    weight = pl.BlockSpec((hidden, width), lambda b: (0, 0), pipeline_mode=pl.Buffered(1))
    term, d_gate, d_up, act, d_gate9, d_up9, act9, x9, dy9 = pl.pallas_call(
        unit_kernel,
        grid=(blocks,),
        in_specs=[split((rows, message)), weight, weight, weight],
        out_specs=[split((rows, reply))]
        + [split((rows, hidden))] * 3
        + [split((rows9, hidden))] * 3
        + [split((rows9, width))] * 2,
        out_shape=[jax.ShapeDtypeStruct((slots, reply), BF)]
        + [jax.ShapeDtypeStruct((slots, hidden), BF)] * 3
        + [jax.ShapeDtypeStruct((devices, hidden), BF)] * 3
        + [jax.ShapeDtypeStruct((devices, width), BF)] * 2,
        compiler_params=limits(60),
        name="unit_terms",
    )(got, gate_t, up_t, down)

    returned = lax.all_to_all(
        term.reshape(devices, LOW, reply), AXES, split_axis=0, concat_axis=0, tiled=True
    ).reshape(slots, reply)

    x8, dy8 = got[:, :width], got[:, width : 2 * width]
    grad_gate = (dot(x8, d_gate, TN) + dot(x9, d_gate9, TN)).astype(BF)
    grad_up = (dot(x8, d_up, TN) + dot(x9, d_up9, TN)).astype(BF)
    grad_down = (dot(act, dy8, TN) + dot(act9, dy9, TN)).astype(BF)

    blocks = 4
    grad_tokens, grad_gates = pl.pallas_call(
        lambda *refs: collect_kernel(halves, *refs),
        grid=(blocks,),
        in_specs=[whole((count, top)), whole((count, top)), split((slots // blocks, reply))],
        out_specs=[whole((count, width)), whole((count, top))],
        out_shape=[
            jax.ShapeDtypeStruct((count, width), BF),
            jax.ShapeDtypeStruct((count, top), F32),
        ],
        scratch_shapes=[pltpu.VMEM((count, width), F32), pltpu.VMEM((count, 128), F32)],
        compiler_params=limits(48),
        name="collect_rows",
    )(expert_ids, gate_weights, returned)
    return grad_tokens, grad_gates, grad_gate[None], grad_up[None], grad_down[None]


def solution(mesh):
    row = P(AXES, None)
    unit = P(AXES, None, None)
    return jax.shard_map(
        local,
        mesh=mesh,
        in_specs=(row, row, row, row, unit, unit, unit),
        out_specs=(row, row, unit, unit, unit),
        check_vma=False,
    )
```

```python
import jax
import jax.numpy as jnp
from jax import lax
from jax.experimental import pallas as pl
from jax.experimental.pallas import tpu as pltpu
from jax.sharding import PartitionSpec as P

LOW = 8
BF = jnp.bfloat16
F32 = jnp.float32
AXES = ("node", "local")
NT = (((1,), (1,)), ((), ()))
TN = (((0,), (0,)), ((), ()))


def dot(a, b, dims=(((1,), (0,)), ((), ()))):
    return lax.dot_general(a, b, dims, preferred_element_type=F32)


def row_tables(ids, first, rows, halves):
    tokens = ids.shape[1]
    slot = lax.broadcasted_iota(jnp.int32, (rows, tokens), 0)
    expert = first + slot // (halves * LOW)
    row = slot % LOW
    hit = jnp.zeros((rows, tokens), F32)
    for k in range(ids.shape[0]):
        hit = hit + jnp.where(ids[k : k + 1, :] == expert, 1.0, 0.0)
    before = lax.broadcasted_iota(jnp.int32, (tokens, tokens), 0) < lax.broadcasted_iota(
        jnp.int32, (tokens, tokens), 1
    )
    rank = dot(hit.astype(BF), jnp.where(before, 1.0, 0.0).astype(BF)).astype(jnp.int32)
    return expert, row, hit, rank


def pack_kernel(halves, ids_ref, gates_ref, x_ref, dy_ref, out_ref):
    rows, width = out_ref.shape[0], x_ref.shape[1]
    ids = ids_ref[...]
    gates = gates_ref[...].astype(F32)
    first = pl.program_id(0) * (rows // (halves * LOW))
    expert, row, hit, rank = row_tables(ids, first, rows, halves)
    gate = jnp.zeros(hit.shape, F32)
    for k in range(ids.shape[0]):
        gate = gate + jnp.where(ids[k : k + 1, :] == expert, gates[k : k + 1, :], 0.0)
    low = jnp.where(rank == row, hit, 0.0)
    x, dy = x_ref[...], dy_ref[...]
    out_ref[:, :width] = dot(low.astype(BF), x).astype(BF)
    out_ref[:, width : 2 * width] = dot((low * gate).astype(BF), dy).astype(BF)
    last = jnp.where(rank == LOW, hit, 0.0)
    piece = 2 * width // LOW
    masks, pieces = [], []
    for i in range(LOW):
        at = i * piece
        source, weight = (x, last) if at < width else (dy, last * gate)
        masks.append(jnp.where(row == i, weight, 0.0).astype(BF))
        pieces.append(source[:, at % width : at % width + piece])
    out_ref[:, 2 * width :] = dot(
        jnp.concatenate(masks, 1), jnp.concatenate(pieces, 0)
    ).astype(BF)


def piece_table(sources):
    shape = (sources * LOW, sources * LOW)
    a = lax.broadcasted_iota(jnp.int32, shape, 0)
    b = lax.broadcasted_iota(jnp.int32, shape, 1)
    return jnp.where((a % sources) * LOW + a // sources == b, 1.0, 0.0).astype(BF)


def nine_rows(got9_ref, rows9):
    block = 32
    table = piece_table(block)
    x9, dy9 = [], []
    for first in range(0, rows9, block):
        pieces = dot(table, got9_ref[first * LOW : (first + block) * LOW, :]).astype(BF)
        pieces = [pieces[i * block : (i + 1) * block] for i in range(LOW)]
        x9.append(jnp.concatenate(pieces[: LOW // 2], 1))
        dy9.append(jnp.concatenate(pieces[LOW // 2 :], 1))
    return jnp.concatenate(x9, 0), jnp.concatenate(dy9, 0)


def unit_rows(x, dy, gate_ref, up_ref, down_ref, dg_ref, du_ref, act_ref):
    pre_gate = dot(gate_ref[...], x, NT)
    pre_up = dot(up_ref[...], x, NT)
    back = dot(down_ref[...], dy, NT)
    sig = jax.nn.sigmoid(pre_gate)
    silu = pre_gate * sig
    act = silu * pre_up
    part = jnp.sum(act * back, axis=0, keepdims=True)
    d_gate = (back * pre_up * sig * (1.0 + pre_gate * (1.0 - sig))).astype(BF)
    d_up = (back * silu).astype(BF)
    dg_ref[...], du_ref[...], act_ref[...] = d_gate, d_up, act.astype(BF)
    term = dot(d_gate, gate_ref[...], TN) + dot(d_up, up_ref[...], TN)
    return term.astype(BF), jnp.transpose(jnp.broadcast_to(part, (128, part.shape[1])))


def unit_kernel(
    got_ref, got9_ref, gate_ref, up_ref, down_ref,
    back_ref, dg_ref, du_ref, act_ref, dg9_ref, du9_ref, act9_ref, x9_ref, dy9_ref, tail_ref,
):
    rows, width = got_ref.shape[0], gate_ref.shape[1]
    rows9 = x9_ref.shape[0]
    piece = width // LOW
    block = 32
    step = pl.program_id(0)

    @pl.when(step == 0)
    def _():
        x9, dy9 = nine_rows(got9_ref, rows9)
        x9_ref[...], dy9_ref[...] = x9, dy9
        term, part = unit_rows(x9, dy9, gate_ref, up_ref, down_ref, dg9_ref, du9_ref, act9_ref)
        table = piece_table(block)
        lane = lax.broadcasted_iota(jnp.int32, (block, 128), 1)
        for first in range(0, rows9, block):
            at = slice(first, first + block)
            to = slice(first * LOW, (first + block) * LOW)
            pieces = [term[at, i * piece : (i + 1) * piece] for i in range(LOW)]
            tail_ref[to, :piece] = dot(table, jnp.concatenate(pieces, 0), TN).astype(BF)
            part9 = jnp.where(lane == 1, part[at], 0.0).astype(BF)
            tail_ref[to, piece:] = dot(table[:block], part9, TN).astype(BF)

    term, part = unit_rows(
        got_ref[:, :width], got_ref[:, width : 2 * width],
        gate_ref, up_ref, down_ref, dg_ref, du_ref, act_ref,
    )
    here = pl.ds(pl.multiple_of(step * rows, rows), rows)
    back_ref[:, :width] = term
    back_ref[:, width : width + piece] = tail_ref[here, :piece]
    lane = lax.broadcasted_iota(jnp.int32, (rows, 128), 1)
    back_ref[:, width + piece :] = jnp.where(
        lane == 0, part, tail_ref[here, piece:].astype(F32)
    ).astype(BF)


def collect_kernel(halves, ids_ref, gates_ref, back_ref, out_ref, gg_ref, sum_ref, part_ref):
    rows, width = back_ref.shape[0], out_ref.shape[1]
    step = pl.program_id(0)
    ids = ids_ref[...]
    top = ids.shape[0]
    first = step * (rows // (halves * LOW))
    expert, row, hit, rank = row_tables(ids, first, rows, halves)
    low = jnp.where(rank == row, hit, 0.0)
    last = jnp.where(rank == LOW, hit, 0.0)

    @pl.when(step == 0)
    def _():
        sum_ref[...] = jnp.zeros_like(sum_ref)
        part_ref[...] = jnp.zeros_like(part_ref)

    piece = width // LOW
    pieces = back_ref[:, width : width + piece]
    total = dot(low.astype(BF), back_ref[:, :width], TN)
    for i in range(LOW):
        mask = jnp.where(row == i, last, 0.0).astype(BF)
        at = slice(i * piece, (i + 1) * piece)
        sum_ref[:, at] += total[:, at] + dot(mask, pieces, TN)
    parts = back_ref[:, width + piece :].astype(F32)
    mine = low * parts[:, 0:1] + jnp.where(row == 0, last, 0.0) * parts[:, 1:2]
    for k in range(top):
        part_ref[k : k + 1, :] += jnp.sum(
            jnp.where(ids[k : k + 1, :] == expert, mine, 0.0), axis=0, keepdims=True
        )

    @pl.when(step == pl.num_programs(0) - 1)
    def _():
        out_ref[...] = sum_ref[...].astype(BF)
        gg_ref[...] = part_ref[:top, :] / gates_ref[...].astype(F32)


def whole(shape):
    return pl.BlockSpec(shape, lambda b: (0,) * len(shape))


def split(shape):
    return pl.BlockSpec(shape, lambda b: (b,) + (0,) * (len(shape) - 1))


def limits(mib):
    return pltpu.CompilerParams(
        dimension_semantics=("arbitrary",), vmem_limit_bytes=mib * 2**20
    )


def local(tokens, cotangent, gate_weights, expert_ids, gate_proj, up_proj, down_proj):
    devices = lax.axis_size("node") * lax.axis_size("local")
    count, width = tokens.shape
    hidden = down_proj.shape[1]
    halves = 2
    experts = devices // halves
    slots = devices * LOW
    top = expert_ids.shape[1]
    ids_t, gates_t = jnp.swapaxes(expert_ids, 0, 1), jnp.swapaxes(gate_weights, 0, 1)

    blocks = 4
    message = 2 * width + 2 * width // LOW
    sent = pl.pallas_call(
        lambda *refs: pack_kernel(halves, *refs),
        grid=(blocks,),
        in_specs=[
            whole((top, count)), whole((top, count)), whole((count, width)), whole((count, width)),
        ],
        out_specs=split((slots // blocks, message)),
        out_shape=jax.ShapeDtypeStruct((slots, message), BF),
        compiler_params=limits(48),
        name="pack_rows",
    )(ids_t, gates_t, tokens, cotangent)

    got = lax.all_to_all(
        sent.reshape(devices, LOW, message), AXES, split_axis=0, concat_axis=0, tiled=True
    ).reshape(slots, message)

    gate_t = jnp.swapaxes(gate_proj[0], 0, 1)
    up_t = jnp.swapaxes(up_proj[0], 0, 1)
    down = down_proj[0]
    blocks = 2
    rows = slots // blocks
    piece = width // LOW
    reply = width + piece + 128
    gate_t, up_t, down = (
        pltpu.with_memory_space_constraint(w, pltpu.VMEM) for w in (gate_t, up_t, down)
    )
    weight = pl.BlockSpec(memory_space=pltpu.VMEM)
    units = pl.BlockSpec((hidden, rows), lambda b: (0, b))
    term, d_gate, d_up, act, d_gate9, d_up9, act9, x9, dy9 = pl.pallas_call(
        unit_kernel,
        grid=(blocks,),
        in_specs=[
            split((rows, message)),
            pl.BlockSpec((slots, 2 * piece), lambda b: (0, LOW)),
            weight, weight, weight,
        ],
        out_specs=[split((rows, reply))]
        + [units] * 3
        + [whole((hidden, devices))] * 3
        + [whole((devices, width))] * 2,
        out_shape=[jax.ShapeDtypeStruct((slots, reply), BF)]
        + [jax.ShapeDtypeStruct((hidden, slots), BF)] * 3
        + [jax.ShapeDtypeStruct((hidden, devices), BF)] * 3
        + [jax.ShapeDtypeStruct((devices, width), BF)] * 2,
        scratch_shapes=[pltpu.VMEM((slots, piece + 128), BF)],
        compiler_params=limits(48),
        name="unit_terms",
    )(got, got, gate_t, up_t, down)

    returned = lax.all_to_all(
        term.reshape(devices, LOW, reply), AXES, split_axis=0, concat_axis=0, tiled=True
    ).reshape(slots, reply)

    x8, dy8 = got[:, :width], got[:, width : 2 * width]
    grad_gate = (dot(d_gate, x8) + dot(d_gate9, x9)).astype(BF)
    grad_up = (dot(d_up, x8) + dot(d_up9, x9)).astype(BF)
    grad_gate, grad_up = jnp.swapaxes(grad_gate, 0, 1), jnp.swapaxes(grad_up, 0, 1)
    grad_down = (dot(act, dy8) + dot(act9, dy9)).astype(BF)

    blocks = 4
    grad_tokens, grad_gates = pl.pallas_call(
        lambda *refs: collect_kernel(halves, *refs),
        grid=(blocks,),
        in_specs=[whole((top, count)), whole((top, count)), split((slots // blocks, reply))],
        out_specs=[whole((count, width)), whole((top, count))],
        out_shape=[
            jax.ShapeDtypeStruct((count, width), BF),
            jax.ShapeDtypeStruct((top, count), F32),
        ],
        scratch_shapes=[pltpu.VMEM((count, width), F32), pltpu.VMEM((8, count), F32)],
        compiler_params=limits(48),
        name="collect_rows",
    )(ids_t, gates_t, returned)
    grad_gates = jnp.swapaxes(grad_gates, 0, 1)
    return grad_tokens, grad_gates, grad_gate[None], grad_up[None], grad_down[None]


def solution(mesh):
    row = P(AXES, None)
    unit = P(AXES, None, None)
    return jax.shard_map(
        local,
        mesh=mesh,
        in_specs=(row, row, row, row, unit, unit, unit),
        out_specs=(row, row, unit, unit, unit),
        check_vma=False,
    )
```

```python
import jax
import jax.numpy as jnp
from jax import lax
from jax.experimental import pallas as pl
from jax.experimental.pallas import tpu as pltpu
from jax.sharding import PartitionSpec as P

LOW = 8
BF = jnp.bfloat16
F32 = jnp.float32
AXES = ("node", "local")
NT = (((1,), (1,)), ((), ()))
TN = (((0,), (0,)), ((), ()))


def dot(a, b, dims=(((1,), (0,)), ((), ()))):
    return lax.dot_general(a, b, dims, preferred_element_type=F32)


def row_tables(ids, first, rows, halves):
    tokens = ids.shape[1]
    slot = lax.broadcasted_iota(jnp.int32, (rows, tokens), 0)
    expert = first + slot // (halves * LOW)
    row = slot % LOW
    hit = jnp.zeros((rows, tokens), F32)
    for k in range(ids.shape[0]):
        hit = hit + jnp.where(ids[k : k + 1, :] == expert, 1.0, 0.0)
    before = lax.broadcasted_iota(jnp.int32, (tokens, tokens), 0) < lax.broadcasted_iota(
        jnp.int32, (tokens, tokens), 1
    )
    rank = dot(hit.astype(BF), jnp.where(before, 1.0, 0.0).astype(BF)).astype(jnp.int32)
    return expert, row, hit, rank


def pack_kernel(halves, ids_ref, gates_ref, x_ref, dy_ref, out_ref):
    rows, width = out_ref.shape[0], x_ref.shape[1]
    ids = ids_ref[...]
    gates = gates_ref[...].astype(F32)
    first = pl.program_id(0) * (rows // (halves * LOW))
    expert, row, hit, rank = row_tables(ids, first, rows, halves)
    gate = jnp.zeros(hit.shape, F32)
    for k in range(ids.shape[0]):
        gate = gate + jnp.where(ids[k : k + 1, :] == expert, gates[k : k + 1, :], 0.0)
    low = jnp.where(rank == row, hit, 0.0)
    x, dy = x_ref[...], dy_ref[...]
    out_ref[:, :width] = dot(low.astype(BF), x).astype(BF)
    out_ref[:, width : 2 * width] = dot((low * gate).astype(BF), dy).astype(BF)
    last = jnp.where(rank == LOW, hit, 0.0)
    piece = 2 * width // LOW
    masks, pieces = [], []
    for i in range(LOW):
        at = i * piece
        source, weight = (x, last) if at < width else (dy, last * gate)
        masks.append(jnp.where(row == i, weight, 0.0).astype(BF))
        pieces.append(source[:, at % width : at % width + piece])
    out_ref[:, 2 * width :] = dot(
        jnp.concatenate(masks, 1), jnp.concatenate(pieces, 0)
    ).astype(BF)


def piece_table(sources):
    shape = (sources * LOW, sources * LOW)
    a = lax.broadcasted_iota(jnp.int32, shape, 0)
    b = lax.broadcasted_iota(jnp.int32, shape, 1)
    return jnp.where((a % sources) * LOW + a // sources == b, 1.0, 0.0).astype(BF)


def nine_rows(got_ref, at, rows9):
    block = 32
    table = piece_table(block)
    x9, dy9 = [], []
    for first in range(0, rows9, block):
        pieces = dot(table, got_ref[first * LOW : (first + block) * LOW, at:]).astype(BF)
        pieces = [pieces[i * block : (i + 1) * block] for i in range(LOW)]
        x9.append(jnp.concatenate(pieces[: LOW // 2], 1))
        dy9.append(jnp.concatenate(pieces[LOW // 2 :], 1))
    return jnp.concatenate(x9, 0), jnp.concatenate(dy9, 0)


def unit_rows(x, dy, gate_ref, up_ref, down_ref, dg_ref, du_ref, act_ref):
    pre_gate = dot(gate_ref[...], x, NT)
    pre_up = dot(up_ref[...], x, NT)
    back = dot(down_ref[...], dy, NT)
    sig = jax.nn.sigmoid(pre_gate)
    silu = pre_gate * sig
    act = silu * pre_up
    part = jnp.sum(act * back, axis=0, keepdims=True)
    d_gate = (back * pre_up * sig * (1.0 + pre_gate * (1.0 - sig))).astype(BF)
    d_up = (back * silu).astype(BF)
    dg_ref[...], du_ref[...], act_ref[...] = d_gate, d_up, act.astype(BF)
    term = dot(d_gate, gate_ref[...], TN) + dot(d_up, up_ref[...], TN)
    return term.astype(BF), jnp.transpose(jnp.broadcast_to(part, (128, part.shape[1])))


def unit_kernel(
    got_ref, gate_ref, up_ref, down_ref,
    back_ref, dg_ref, du_ref, act_ref, dg9_ref, du9_ref, act9_ref, x9_ref, dy9_ref, tail_ref,
):
    rows, width = back_ref.shape[0], gate_ref.shape[1]
    rows9 = x9_ref.shape[0]
    piece = width // LOW
    block = 32
    step = pl.program_id(0)

    @pl.when(step == 0)
    def _():
        x9, dy9 = nine_rows(got_ref, 2 * width, rows9)
        x9_ref[...], dy9_ref[...] = x9, dy9
        term, part = unit_rows(x9, dy9, gate_ref, up_ref, down_ref, dg9_ref, du9_ref, act9_ref)
        table = piece_table(block)
        lane = lax.broadcasted_iota(jnp.int32, (block, 128), 1)
        for first in range(0, rows9, block):
            at = slice(first, first + block)
            to = slice(first * LOW, (first + block) * LOW)
            pieces = [term[at, i * piece : (i + 1) * piece] for i in range(LOW)]
            tail_ref[to, :piece] = dot(table, jnp.concatenate(pieces, 0), TN).astype(BF)
            part9 = jnp.where(lane == 1, part[at], 0.0).astype(BF)
            tail_ref[to, piece:] = dot(table[:block], part9, TN).astype(BF)

    here = pl.ds(pl.multiple_of(step * rows, rows), rows)
    term, part = unit_rows(
        got_ref[here, :width], got_ref[here, width : 2 * width],
        gate_ref, up_ref, down_ref, dg_ref, du_ref, act_ref,
    )
    back_ref[:, :width] = term
    back_ref[:, width : width + piece] = tail_ref[here, :piece]
    lane = lax.broadcasted_iota(jnp.int32, (rows, 128), 1)
    back_ref[:, width + piece :] = jnp.where(
        lane == 0, part, tail_ref[here, piece:].astype(F32)
    ).astype(BF)


def collect_kernel(halves, ids_ref, gates_ref, back_ref, out_ref, gg_ref):
    rows, width = back_ref.shape[0], out_ref.shape[1]
    ids = ids_ref[...]
    top, count = ids.shape
    expert, row, hit, rank = row_tables(ids, 0, rows, halves)
    low = jnp.where(rank == row, hit, 0.0)
    last = jnp.where(rank == LOW, hit, 0.0)
    piece = width // LOW
    masks = jnp.concatenate(
        [jnp.where(row == i, last, 0.0).astype(BF) for i in range(LOW)], 1
    )
    pieces = dot(masks, back_ref[:, width : width + piece], TN)
    low_t = low.astype(BF)
    for i in range(LOW):
        at = slice(i * piece, (i + 1) * piece)
        total = dot(low_t, back_ref[:, at], TN) + pieces[i * count : (i + 1) * count]
        out_ref[:, at] = total.astype(BF)
    parts = back_ref[:, width + piece :].astype(F32)
    mine = low * parts[:, 0:1] + jnp.where(row == 0, last, 0.0) * parts[:, 1:2]
    for k in range(top):
        part = jnp.sum(
            jnp.where(ids[k : k + 1, :] == expert, mine, 0.0), axis=0, keepdims=True
        )
        gg_ref[k : k + 1, :] = part / gates_ref[k : k + 1, :].astype(F32)


def whole(shape):
    return pl.BlockSpec(shape, lambda b: (0,) * len(shape))


def split(shape):
    return pl.BlockSpec(shape, lambda b: (b,) + (0,) * (len(shape) - 1))


def limits(mib):
    return pltpu.CompilerParams(
        dimension_semantics=("arbitrary",), vmem_limit_bytes=mib * 2**20
    )


def local(tokens, cotangent, gate_weights, expert_ids, gate_proj, up_proj, down_proj):
    devices = lax.axis_size("node") * lax.axis_size("local")
    count, width = tokens.shape
    hidden = down_proj.shape[1]
    halves = 2
    experts = devices // halves
    slots = devices * LOW
    top = expert_ids.shape[1]
    ids_t, gates_t = jnp.swapaxes(expert_ids, 0, 1), jnp.swapaxes(gate_weights, 0, 1)

    blocks = 4
    message = 2 * width + 2 * width // LOW
    sent = pl.pallas_call(
        lambda *refs: pack_kernel(halves, *refs),
        grid=(blocks,),
        in_specs=[
            whole((top, count)), whole((top, count)), whole((count, width)), whole((count, width)),
        ],
        out_specs=split((slots // blocks, message)),
        out_shape=jax.ShapeDtypeStruct((slots, message), BF),
        compiler_params=limits(60),
        name="pack_rows",
    )(ids_t, gates_t, tokens, cotangent)

    got = lax.all_to_all(
        sent.reshape(devices, LOW, message), AXES, split_axis=0, concat_axis=0, tiled=True
    ).reshape(slots, message)

    gate_t = jnp.swapaxes(gate_proj[0], 0, 1)
    up_t = jnp.swapaxes(up_proj[0], 0, 1)
    down = down_proj[0]
    blocks = 2
    rows = slots // blocks
    piece = width // LOW
    reply = width + piece + 128
    gate_t, up_t, down, held = (
        pltpu.with_memory_space_constraint(w, pltpu.VMEM) for w in (gate_t, up_t, down, got)
    )
    weight = pl.BlockSpec(memory_space=pltpu.VMEM)
    units = pl.BlockSpec((hidden, rows), lambda b: (0, b))
    term, d_gate, d_up, act, d_gate9, d_up9, act9, x9, dy9 = pl.pallas_call(
        unit_kernel,
        grid=(blocks,),
        in_specs=[
            weight, weight, weight, weight,
        ],
        out_specs=[split((rows, reply))]
        + [units] * 3
        + [whole((hidden, devices))] * 3
        + [whole((devices, width))] * 2,
        out_shape=[jax.ShapeDtypeStruct((slots, reply), BF)]
        + [jax.ShapeDtypeStruct((hidden, slots), BF)] * 3
        + [jax.ShapeDtypeStruct((hidden, devices), BF)] * 3
        + [jax.ShapeDtypeStruct((devices, width), BF)] * 2,
        scratch_shapes=[pltpu.VMEM((slots, piece + 128), BF)],
        compiler_params=limits(36),
        name="unit_terms",
    )(held, gate_t, up_t, down)

    returned = lax.all_to_all(
        term.reshape(devices, LOW, reply), AXES, split_axis=0, concat_axis=0, tiled=True
    ).reshape(slots, reply)

    x8, dy8 = got[:, :width], got[:, width : 2 * width]
    grad_gate = (dot(d_gate, x8) + dot(d_gate9, x9)).astype(BF)
    grad_up = (dot(d_up, x8) + dot(d_up9, x9)).astype(BF)
    grad_gate, grad_up = jnp.swapaxes(grad_gate, 0, 1), jnp.swapaxes(grad_up, 0, 1)
    grad_down = (dot(act, dy8) + dot(act9, dy9)).astype(BF)

    held = pltpu.with_memory_space_constraint(returned, pltpu.VMEM)
    grad_tokens, grad_gates = pl.pallas_call(
        lambda *refs: collect_kernel(halves, *refs),
        in_specs=[pl.BlockSpec(memory_space=pltpu.VMEM)] * 3,
        out_specs=[pl.BlockSpec(memory_space=pltpu.VMEM)] * 2,
        out_shape=[
            jax.ShapeDtypeStruct((count, width), BF),
            jax.ShapeDtypeStruct((top, count), F32),
        ],
        compiler_params=pltpu.CompilerParams(vmem_limit_bytes=32 * 2**20),
        name="collect_rows",
    )(ids_t, gates_t, held)
    grad_gates = jnp.swapaxes(grad_gates, 0, 1)
    return grad_tokens, grad_gates, grad_gate[None], grad_up[None], grad_down[None]


def solution(mesh):
    row = P(AXES, None)
    unit = P(AXES, None, None)
    return jax.shard_map(
        local,
        mesh=mesh,
        in_specs=(row, row, row, row, unit, unit, unit),
        out_specs=(row, row, unit, unit, unit),
        check_vma=False,
    )
```

```python
import jax
import jax.numpy as jnp
from jax import lax
from jax.experimental import pallas as pl
from jax.experimental.pallas import tpu as pltpu
from jax.sharding import PartitionSpec as P

LOW = 8
BF = jnp.bfloat16
F32 = jnp.float32
AXES = ("node", "local")
NT = (((1,), (1,)), ((), ()))
TN = (((0,), (0,)), ((), ()))


def dot(a, b, dims=(((1,), (0,)), ((), ()))):
    return lax.dot_general(a, b, dims, preferred_element_type=F32)


def row_tables(ids, first, rows, halves):
    tokens = ids.shape[1]
    slot = lax.broadcasted_iota(jnp.int32, (rows, tokens), 0)
    expert = first + slot // (halves * LOW)
    row = slot % LOW
    hit = jnp.zeros((rows, tokens), F32)
    for k in range(ids.shape[0]):
        hit = hit + jnp.where(ids[k : k + 1, :] == expert, 1.0, 0.0)
    before = lax.broadcasted_iota(jnp.int32, (tokens, tokens), 0) < lax.broadcasted_iota(
        jnp.int32, (tokens, tokens), 1
    )
    rank = dot(hit.astype(BF), jnp.where(before, 1.0, 0.0).astype(BF)).astype(jnp.int32)
    return expert, row, hit, rank


def pack_kernel(halves, ids_ref, gates_ref, x_ref, dy_ref, out_ref):
    rows, width = out_ref.shape[0], x_ref.shape[1]
    ids = ids_ref[...]
    gates = gates_ref[...].astype(F32)
    first = pl.program_id(0) * (rows // (halves * LOW))
    expert, row, hit, rank = row_tables(ids, first, rows, halves)
    gate = jnp.zeros(hit.shape, F32)
    for k in range(ids.shape[0]):
        gate = gate + jnp.where(ids[k : k + 1, :] == expert, gates[k : k + 1, :], 0.0)
    low = jnp.where(rank == row, hit, 0.0)
    x, dy = x_ref[...], dy_ref[...]
    out_ref[:, :width] = dot(low.astype(BF), x).astype(BF)
    out_ref[:, width : 2 * width] = dot((low * gate).astype(BF), dy).astype(BF)
    last = jnp.where(rank == LOW, hit, 0.0)
    piece = 2 * width // LOW
    masks, pieces = [], []
    for i in range(LOW):
        at = i * piece
        source, weight = (x, last) if at < width else (dy, last * gate)
        masks.append(jnp.where(row == i, weight, 0.0).astype(BF))
        pieces.append(source[:, at % width : at % width + piece])
    out_ref[:, 2 * width :] = dot(
        jnp.concatenate(masks, 1), jnp.concatenate(pieces, 0)
    ).astype(BF)


def piece_table(sources):
    shape = (sources * LOW, sources * LOW)
    a = lax.broadcasted_iota(jnp.int32, shape, 0)
    b = lax.broadcasted_iota(jnp.int32, shape, 1)
    return jnp.where((a % sources) * LOW + a // sources == b, 1.0, 0.0).astype(BF)


def nine_rows(got_ref, at, rows9):
    block = 32
    table = piece_table(block)
    x9, dy9 = [], []
    for first in range(0, rows9, block):
        pieces = dot(table, got_ref[first * LOW : (first + block) * LOW, at:]).astype(BF)
        pieces = [pieces[i * block : (i + 1) * block] for i in range(LOW)]
        x9.append(jnp.concatenate(pieces[: LOW // 2], 1))
        dy9.append(jnp.concatenate(pieces[LOW // 2 :], 1))
    return jnp.concatenate(x9, 0), jnp.concatenate(dy9, 0)


def unit_kernel(
    got_ref, gate_ref, up_ref, down_ref,
    back_hbm, dg_hbm, du_hbm, act_hbm, dg9_ref, du9_ref, act9_ref, x9_ref, dy9_ref,
    back_ref, dg_ref, du_ref, act_ref, done,
):
    width = gate_ref.shape[1]
    blocks, _, rows = dg_ref.shape
    sources = x9_ref.shape[0]
    piece = width // LOW
    tail = width + piece
    copies = []

    def send(source, target):
        copy = pltpu.make_async_copy(source, target, done.at[len(copies)])
        copy.start()
        copies.append(copy)

    def activations(x, dy):
        pre_gate = dot(gate_ref[...], x, NT)
        pre_up = dot(up_ref[...], x, NT)
        back = dot(down_ref[...], dy, NT)
        sig = jax.nn.sigmoid(pre_gate)
        silu = pre_gate * sig
        act = silu * pre_up
        part = jnp.sum(act * back, axis=0, keepdims=True)
        d_gate = (back * pre_up * (sig + silu * (1.0 - sig))).astype(BF)
        d_up = (back * silu).astype(BF)
        part = jnp.transpose(jnp.broadcast_to(part, (128, part.shape[1])))
        return d_gate, d_up, act.astype(BF), part

    def terms(d_gate, d_up):
        return (dot(d_gate, gate_ref[...], TN) + dot(d_up, up_ref[...], TN)).astype(BF)

    def start_block(i):
        at = slice(i * rows, (i + 1) * rows)
        d_gate, d_up, act, part = activations(got_ref[at, :width], got_ref[at, width : 2 * width])
        for held, out, value in (
            (dg_ref, dg_hbm, d_gate), (du_ref, du_hbm, d_up), (act_ref, act_hbm, act),
        ):
            held[i] = value
            send(held.at[i], out.at[:, pl.ds(i * rows, rows)])
        lane = lax.broadcasted_iota(jnp.int32, (rows, 128), 1)
        back_ref[at, tail:] = jnp.where(lane == 0, part, 0.0).astype(BF)
        return d_gate, d_up

    def end_block(i, d_gate, d_up):
        back_ref[i * rows : (i + 1) * rows, :width] = terms(d_gate, d_up)
        here = (pl.ds(i * rows, rows), pl.ds(0, width))
        send(back_ref.at[here], back_hbm.at[here])

    last = start_block(0)
    for i in range(1, blocks):
        now = start_block(i)
        end_block(i - 1, *last)
        last = now

    x9, dy9 = nine_rows(got_ref, 2 * width, sources)
    x9_ref[...], dy9_ref[...] = x9, dy9
    d_gate, d_up, act, part = activations(x9, dy9)
    dg9_ref[...], du9_ref[...], act9_ref[...] = d_gate, d_up, act
    end_block(blocks - 1, *last)
    term = terms(d_gate, d_up)
    block = 32
    table = piece_table(block)
    lane = lax.broadcasted_iota(jnp.int32, (block, 128), 1)
    for first in range(0, sources, block):
        at = slice(first, first + block)
        to = slice(first * LOW, (first + block) * LOW)
        pieces = [term[at, i * piece : (i + 1) * piece] for i in range(LOW)]
        back_ref[to, width:tail] = dot(table, jnp.concatenate(pieces, 0), TN).astype(BF)
        part9 = jnp.where(lane == 1, part[at], 0.0).astype(BF)
        part9 = dot(table[:block], part9, TN)
        back_ref[to, tail:] = (back_ref[to, tail:].astype(F32) + part9).astype(BF)
    here = (slice(None), pl.ds(width, piece + 128))
    send(back_ref.at[here], back_hbm.at[here])
    for copy in copies:
        copy.wait()


def collect_kernel(halves, ids_ref, gates_ref, back_ref, out_ref, gg_ref, sum_ref, part_ref):
    rows, width = back_ref.shape[0], out_ref.shape[1]
    step = pl.program_id(0)
    ids = ids_ref[...]
    top, count = ids.shape
    first = step * (rows // (halves * LOW))
    expert, row, hit, rank = row_tables(ids, first, rows, halves)
    low = jnp.where(rank == row, hit, 0.0)
    last = jnp.where(rank == LOW, hit, 0.0)
    piece = width // LOW

    @pl.when(step == 0)
    def _():
        sum_ref[...] = jnp.zeros_like(sum_ref)
        part_ref[...] = jnp.zeros_like(part_ref)

    low_t, last_t = jnp.transpose(low), jnp.transpose(last)
    row_t = lax.broadcasted_iota(jnp.int32, (count, rows), 1) % LOW
    masks = jnp.concatenate(
        [jnp.where(row_t == i, last_t, 0.0).astype(BF) for i in range(LOW)], 0
    )
    pieces = dot(masks, back_ref[:, width : width + piece])
    total = dot(low_t.astype(BF), back_ref[:, :width])
    for i in range(LOW):
        at = slice(i * piece, (i + 1) * piece)
        sum_ref[:, at] += total[:, at] + pieces[i * count : (i + 1) * count]
    parts = back_ref[:, width + piece :].astype(F32)
    mine = low * parts[:, 0:1] + jnp.where(row == 0, last, 0.0) * parts[:, 1:2]
    for k in range(top):
        part_ref[k : k + 1, :] += jnp.sum(
            jnp.where(ids[k : k + 1, :] == expert, mine, 0.0), axis=0, keepdims=True
        )

    @pl.when(step == pl.num_programs(0) - 1)
    def _():
        out_ref[...] = sum_ref[...].astype(BF)
        gg_ref[...] = part_ref[:top, :] / gates_ref[...].astype(F32)


def whole(shape):
    return pl.BlockSpec(shape, lambda b: (0,) * len(shape))


def split(shape):
    return pl.BlockSpec(shape, lambda b: (b,) + (0,) * (len(shape) - 1))


def limits(mib):
    return pltpu.CompilerParams(
        dimension_semantics=("arbitrary",), vmem_limit_bytes=mib * 2**20
    )


def local(tokens, cotangent, gate_weights, expert_ids, gate_proj, up_proj, down_proj):
    devices = lax.axis_size("node") * lax.axis_size("local")
    count, width = tokens.shape
    hidden = down_proj.shape[1]
    halves = 2
    experts = devices // halves
    slots = devices * LOW
    top = expert_ids.shape[1]
    ids_t, gates_t = jnp.swapaxes(expert_ids, 0, 1), jnp.swapaxes(gate_weights, 0, 1)

    blocks = 4
    message = 2 * width + 2 * width // LOW
    sent = pl.pallas_call(
        lambda *refs: pack_kernel(halves, *refs),
        grid=(blocks,),
        in_specs=[
            whole((top, count)), whole((top, count)), whole((count, width)), whole((count, width)),
        ],
        out_specs=split((slots // blocks, message)),
        out_shape=jax.ShapeDtypeStruct((slots, message), BF),
        compiler_params=limits(60),
        name="pack_rows",
    )(ids_t, gates_t, tokens, cotangent)

    got = lax.all_to_all(
        sent.reshape(devices, LOW, message), AXES, split_axis=0, concat_axis=0, tiled=True
    ).reshape(slots, message)

    gate_t = jnp.swapaxes(gate_proj[0], 0, 1)
    up_t = jnp.swapaxes(up_proj[0], 0, 1)
    down = down_proj[0]
    blocks = 4
    rows = slots // blocks
    piece = width // LOW
    reply = width + piece + 128
    gate_t, up_t, down, held = (
        pltpu.with_memory_space_constraint(w, pltpu.VMEM) for w in (gate_t, up_t, down, got)
    )
    inside = pl.BlockSpec(memory_space=pltpu.VMEM)
    outside = pl.BlockSpec(memory_space=pl.ANY)
    term, d_gate, d_up, act, d_gate9, d_up9, act9, x9, dy9 = pl.pallas_call(
        unit_kernel,
        in_specs=[inside] * 4,
        out_specs=[outside] * 4 + [inside] * 5,
        out_shape=[jax.ShapeDtypeStruct((slots, reply), BF)]
        + [jax.ShapeDtypeStruct((hidden, slots), BF)] * 3
        + [jax.ShapeDtypeStruct((hidden, devices), BF)] * 3
        + [jax.ShapeDtypeStruct((devices, width), BF)] * 2,
        scratch_shapes=[pltpu.VMEM((slots, reply), BF)]
        + [pltpu.VMEM((blocks, hidden, rows), BF)] * 3
        + [pltpu.SemaphoreType.DMA((4 * blocks + 1,))],
        compiler_params=pltpu.CompilerParams(vmem_limit_bytes=40 * 2**20),
        name="unit_terms",
    )(held, gate_t, up_t, down)

    returned = lax.all_to_all(
        term.reshape(devices, LOW, reply), AXES, split_axis=0, concat_axis=0, tiled=True
    ).reshape(slots, reply)

    x8, dy8 = got[:, :width], got[:, width : 2 * width]
    grad_gate = (dot(d_gate, x8) + dot(d_gate9, x9)).astype(BF)
    grad_up = (dot(d_up, x8) + dot(d_up9, x9)).astype(BF)
    grad_gate, grad_up = jnp.swapaxes(grad_gate, 0, 1), jnp.swapaxes(grad_up, 0, 1)
    grad_down = (dot(act, dy8) + dot(act9, dy9)).astype(BF)

    blocks = 2
    grad_tokens, grad_gates = pl.pallas_call(
        lambda *refs: collect_kernel(halves, *refs),
        grid=(blocks,),
        in_specs=[whole((top, count)), whole((top, count)), split((slots // blocks, reply))],
        out_specs=[whole((count, width)), whole((top, count))],
        out_shape=[
            jax.ShapeDtypeStruct((count, width), BF),
            jax.ShapeDtypeStruct((top, count), F32),
        ],
        scratch_shapes=[pltpu.VMEM((count, width), F32), pltpu.VMEM((8, count), F32)],
        compiler_params=limits(48),
        name="collect_rows",
    )(ids_t, gates_t, returned)
    grad_gates = jnp.swapaxes(grad_gates, 0, 1)
    return grad_tokens, grad_gates, grad_gate[None], grad_up[None], grad_down[None]


def solution(mesh):
    row = P(AXES, None)
    unit = P(AXES, None, None)
    return jax.shard_map(
        local,
        mesh=mesh,
        in_specs=(row, row, row, row, unit, unit, unit),
        out_specs=(row, row, unit, unit, unit),
        check_vma=False,
    )
```

```python
import jax
import jax.numpy as jnp
from jax import lax
from jax.experimental import pallas as pl
from jax.experimental.pallas import tpu as pltpu
from jax.sharding import PartitionSpec as P

LOW = 8
BF = jnp.bfloat16
F32 = jnp.float32
AXES = ("node", "local")
ORDER = ("local", "node")
NT = (((1,), (1,)), ((), ()))
TN = (((0,), (0,)), ((), ()))


def dot(a, b, dims=(((1,), (0,)), ((), ()))):
    return lax.dot_general(a, b, dims, preferred_element_type=F32)


def over(a, n):
    assert n & (n - 1) == 0
    return lax.shift_right_logical(a, n.bit_length() - 1), a & (n - 1)


def row_tables(ids, first, rows, sizes):
    tokens = ids.shape[1]
    nodes, members, halves = sizes
    device, row = over(first + lax.broadcasted_iota(jnp.int32, (rows, 1), 0), LOW)
    unit, node = over(device, nodes)
    expert = node * members + over(unit, halves)[0]
    hit = jnp.zeros((rows, tokens), F32)
    for k in range(ids.shape[0]):
        hit = hit + jnp.where(ids[k : k + 1, :] == expert, 1.0, 0.0)
    before = lax.broadcasted_iota(jnp.int32, (tokens, tokens), 0) < lax.broadcasted_iota(
        jnp.int32, (tokens, tokens), 1
    )
    rank = dot(hit.astype(BF), jnp.where(before, 1.0, 0.0).astype(BF)).astype(jnp.int32)
    return expert, row, hit, rank


def pack_kernel(sizes, ids_ref, gates_ref, x_ref, dy_ref, out_ref):
    nodes, members, halves = sizes
    width = x_ref.shape[1]
    run = nodes * LOW
    rows = out_ref.shape[0] // halves
    ids = ids_ref[...]
    gates = gates_ref[...].astype(F32)
    expert, row, hit, rank = row_tables(ids, pl.program_id(0) * rows, rows, (nodes, members, 1))
    gate = jnp.zeros(hit.shape, F32)
    for k in range(ids.shape[0]):
        gate = gate + jnp.where(ids[k : k + 1, :] == expert, gates[k : k + 1, :], 0.0)
    low = jnp.where(rank == row, hit, 0.0)
    x, dy = x_ref[...], dy_ref[...]
    last = jnp.where(rank == LOW, hit, 0.0)
    piece = 2 * width // LOW
    masks, pieces = [], []
    for i in range(LOW):
        at = i * piece
        source, weight = (x, last) if at < width else (dy, last * gate)
        masks.append(jnp.where(row == i, weight, 0.0).astype(BF))
        pieces.append(source[:, at % width : at % width + piece])

    def put(value, to):
        value = value.astype(BF)
        for i in range(rows // run):
            for half in range(halves):
                first = (i * halves + half) * run
                out_ref[first : first + run, to] = value[i * run : (i + 1) * run]

    put(dot(low.astype(BF), x), slice(0, width))
    put(dot((low * gate).astype(BF), dy), slice(width, 2 * width))
    nine = dot(jnp.concatenate(masks, 1), jnp.concatenate(pieces, 0))
    put(nine, slice(2 * width, 2 * width + piece))


def piece_table(sources):
    shape = (sources * LOW, sources * LOW)
    a = lax.broadcasted_iota(jnp.int32, shape, 0)
    b = lax.broadcasted_iota(jnp.int32, shape, 1)
    piece, source = over(a, sources)
    return jnp.where(source * LOW + piece == b, 1.0, 0.0).astype(BF)


def nine_rows(got_ref, at, rows9):
    block = 32
    table = piece_table(block)
    x9, dy9 = [], []
    for first in range(0, rows9, block):
        pieces = dot(table, got_ref[first * LOW : (first + block) * LOW, at:]).astype(BF)
        pieces = [pieces[i * block : (i + 1) * block] for i in range(LOW)]
        x9.append(jnp.concatenate(pieces[: LOW // 2], 1))
        dy9.append(jnp.concatenate(pieces[LOW // 2 :], 1))
    return jnp.concatenate(x9, 0), jnp.concatenate(dy9, 0)


def unit_kernel(
    got_ref, gate_ref, up_ref, down_ref,
    back_hbm, dg_hbm, du_hbm, act_hbm, dg9_ref, du9_ref, act9_ref, x9_ref, dy9_ref,
    back_ref, dg_ref, du_ref, act_ref, done,
):
    width = gate_ref.shape[1]
    blocks, _, rows = dg_ref.shape
    sources = x9_ref.shape[0]
    piece = width // LOW
    tail = width + piece
    copies = []

    def send(source, target):
        copy = pltpu.make_async_copy(source, target, done.at[len(copies)])
        copy.start()
        copies.append(copy)

    def activations(x, dy):
        pre_gate = dot(gate_ref[...], x, NT)
        pre_up = dot(up_ref[...], x, NT)
        back = dot(down_ref[...], dy, NT)
        sig = jax.nn.sigmoid(pre_gate)
        silu = pre_gate * sig
        act = silu * pre_up
        part = jnp.sum(act * back, axis=0, keepdims=True)
        d_gate = (back * pre_up * (sig + silu * (1.0 - sig))).astype(BF)
        d_up = (back * silu).astype(BF)
        part = jnp.transpose(jnp.broadcast_to(part, (128, part.shape[1])))
        return d_gate, d_up, act.astype(BF), part

    def terms(d_gate, d_up):
        return (dot(d_gate, gate_ref[...], TN) + dot(d_up, up_ref[...], TN)).astype(BF)

    def start_block(i):
        at = slice(i * rows, (i + 1) * rows)
        d_gate, d_up, act, part = activations(got_ref[at, :width], got_ref[at, width : 2 * width])
        for held, out, value in (
            (dg_ref, dg_hbm, d_gate), (du_ref, du_hbm, d_up), (act_ref, act_hbm, act),
        ):
            held[i] = value
            send(held.at[i], out.at[:, pl.ds(i * rows, rows)])
        lane = lax.broadcasted_iota(jnp.int32, (rows, 128), 1)
        back_ref[at, tail:] = jnp.where(lane == 0, part, 0.0).astype(BF)
        return d_gate, d_up

    def end_block(i, d_gate, d_up):
        back_ref[i * rows : (i + 1) * rows, :width] = terms(d_gate, d_up)
        here = (pl.ds(i * rows, rows), pl.ds(0, width))
        send(back_ref.at[here], back_hbm.at[here])

    last = start_block(0)
    for i in range(1, blocks):
        now = start_block(i)
        end_block(i - 1, *last)
        last = now

    x9, dy9 = nine_rows(got_ref, 2 * width, sources)
    x9_ref[...], dy9_ref[...] = x9, dy9
    d_gate, d_up, act, part = activations(x9, dy9)
    dg9_ref[...], du9_ref[...], act9_ref[...] = d_gate, d_up, act
    end_block(blocks - 1, *last)
    term = terms(d_gate, d_up)
    block = 32
    table = piece_table(block)
    lane = lax.broadcasted_iota(jnp.int32, (block, 128), 1)
    for first in range(0, sources, block):
        at = slice(first, first + block)
        to = slice(first * LOW, (first + block) * LOW)
        pieces = [term[at, i * piece : (i + 1) * piece] for i in range(LOW)]
        back_ref[to, width:tail] = dot(table, jnp.concatenate(pieces, 0), TN).astype(BF)
        part9 = jnp.where(lane == 1, part[at], 0.0).astype(BF)
        part9 = dot(table[:block], part9, TN)
        back_ref[to, tail:] = (back_ref[to, tail:].astype(F32) + part9).astype(BF)
    here = (slice(None), pl.ds(width, piece + 128))
    send(back_ref.at[here], back_hbm.at[here])
    for copy in copies:
        copy.wait()


def collect_kernel(sizes, ids_ref, gates_ref, back_ref, out_ref, gg_ref, sum_ref, part_ref):
    rows, width = back_ref.shape[0], out_ref.shape[1]
    step = pl.program_id(0)
    ids = ids_ref[...]
    top, count = ids.shape
    first = step * rows
    expert, row, hit, rank = row_tables(ids, first, rows, sizes)
    low = jnp.where(rank == row, hit, 0.0)
    last = jnp.where(rank == LOW, hit, 0.0)
    piece = width // LOW

    @pl.when(step == 0)
    def _():
        sum_ref[...] = jnp.zeros_like(sum_ref)
        part_ref[...] = jnp.zeros_like(part_ref)

    low_t, last_t = jnp.transpose(low), jnp.transpose(last)
    row_t = over(lax.broadcasted_iota(jnp.int32, (1, rows), 1), LOW)[1]
    masks = jnp.concatenate(
        [jnp.where(row_t == i, last_t, 0.0).astype(BF) for i in range(LOW)], 0
    )
    pieces = dot(masks, back_ref[:, width : width + piece])
    total = dot(low_t.astype(BF), back_ref[:, :width])
    for i in range(LOW):
        at = slice(i * piece, (i + 1) * piece)
        sum_ref[:, at] += total[:, at] + pieces[i * count : (i + 1) * count]
    parts = back_ref[:, width + piece :].astype(F32)
    mine = low * parts[:, 0:1] + jnp.where(row == 0, last, 0.0) * parts[:, 1:2]
    for k in range(top):
        part_ref[k : k + 1, :] += jnp.sum(
            jnp.where(ids[k : k + 1, :] == expert, mine, 0.0), axis=0, keepdims=True
        )

    @pl.when(step == pl.num_programs(0) - 1)
    def _():
        out_ref[...] = sum_ref[...].astype(BF)
        gg_ref[...] = part_ref[:top, :] / gates_ref[...].astype(F32)


def whole(shape):
    return pl.BlockSpec(shape, lambda b: (0,) * len(shape))


def split(shape):
    return pl.BlockSpec(shape, lambda b: (b,) + (0,) * (len(shape) - 1))


def limits(mib):
    return pltpu.CompilerParams(
        dimension_semantics=("arbitrary",), vmem_limit_bytes=mib * 2**20
    )


def local(tokens, cotangent, gate_weights, expert_ids, gate_proj, up_proj, down_proj):
    nodes, locals_ = lax.axis_size("node"), lax.axis_size("local")
    devices = nodes * locals_
    count, width = tokens.shape
    hidden = down_proj.shape[1]
    halves = 2
    sizes = (nodes, locals_ // halves, halves)
    slots = devices * LOW
    top = expert_ids.shape[1]
    ids_t, gates_t = jnp.swapaxes(expert_ids, 0, 1), jnp.swapaxes(gate_weights, 0, 1)

    blocks = 4
    message = 2 * width + 2 * width // LOW
    sent = pl.pallas_call(
        lambda *refs: pack_kernel(sizes, *refs),
        grid=(blocks,),
        in_specs=[
            whole((top, count)), whole((top, count)), whole((count, width)), whole((count, width)),
        ],
        out_specs=split((slots // blocks, message)),
        out_shape=jax.ShapeDtypeStruct((slots, message), BF),
        compiler_params=limits(60),
        name="pack_rows",
    )(ids_t, gates_t, tokens, cotangent)

    got = lax.all_to_all(
        sent.reshape(devices, LOW, message), ORDER, split_axis=0, concat_axis=0, tiled=True
    ).reshape(slots, message)

    gate_t = jnp.swapaxes(gate_proj[0], 0, 1)
    up_t = jnp.swapaxes(up_proj[0], 0, 1)
    down = down_proj[0]
    blocks = 4
    rows = slots // blocks
    piece = width // LOW
    reply = width + piece + 128
    gate_t, up_t, down, held = (
        pltpu.with_memory_space_constraint(w, pltpu.VMEM) for w in (gate_t, up_t, down, got)
    )
    inside = pl.BlockSpec(memory_space=pltpu.VMEM)
    outside = pl.BlockSpec(memory_space=pl.ANY)
    term, d_gate, d_up, act, d_gate9, d_up9, act9, x9, dy9 = pl.pallas_call(
        unit_kernel,
        in_specs=[inside] * 4,
        out_specs=[outside] * 4 + [inside] * 5,
        out_shape=[jax.ShapeDtypeStruct((slots, reply), BF)]
        + [jax.ShapeDtypeStruct((hidden, slots), BF)] * 3
        + [jax.ShapeDtypeStruct((hidden, devices), BF)] * 3
        + [jax.ShapeDtypeStruct((devices, width), BF)] * 2,
        scratch_shapes=[pltpu.VMEM((slots, reply), BF)]
        + [pltpu.VMEM((blocks, hidden, rows), BF)] * 3
        + [pltpu.SemaphoreType.DMA((4 * blocks + 1,))],
        compiler_params=pltpu.CompilerParams(vmem_limit_bytes=40 * 2**20),
        name="unit_terms",
    )(held, gate_t, up_t, down)

    returned = lax.all_to_all(
        term.reshape(devices, LOW, reply), ORDER, split_axis=0, concat_axis=0, tiled=True
    ).reshape(slots, reply)

    x8, dy8 = got[:, :width], got[:, width : 2 * width]
    grad_gate = (dot(d_gate, x8) + dot(d_gate9, x9)).astype(BF)
    grad_up = (dot(d_up, x8) + dot(d_up9, x9)).astype(BF)
    grad_gate, grad_up = jnp.swapaxes(grad_gate, 0, 1), jnp.swapaxes(grad_up, 0, 1)
    grad_down = (dot(act, dy8) + dot(act9, dy9)).astype(BF)

    blocks = 2
    grad_tokens, grad_gates = pl.pallas_call(
        lambda *refs: collect_kernel(sizes, *refs),
        grid=(blocks,),
        in_specs=[whole((top, count)), whole((top, count)), split((slots // blocks, reply))],
        out_specs=[whole((count, width)), whole((top, count))],
        out_shape=[
            jax.ShapeDtypeStruct((count, width), BF),
            jax.ShapeDtypeStruct((top, count), F32),
        ],
        scratch_shapes=[pltpu.VMEM((count, width), F32), pltpu.VMEM((8, count), F32)],
        compiler_params=limits(48),
        name="collect_rows",
    )(ids_t, gates_t, returned)
    grad_gates = jnp.swapaxes(grad_gates, 0, 1)
    return grad_tokens, grad_gates, grad_gate[None], grad_up[None], grad_down[None]


def solution(mesh):
    row = P(AXES, None)
    unit = P(AXES, None, None)
    return jax.shard_map(
        local,
        mesh=mesh,
        in_specs=(row, row, row, row, unit, unit, unit),
        out_specs=(row, row, unit, unit, unit),
        check_vma=False,
    )
```

```python
import math

import jax
import jax.numpy as jnp
from jax import lax
from jax.experimental import pallas as pl
from jax.experimental.pallas import tpu as pltpu
from jax.sharding import PartitionSpec as P

LOW = 8
BF = jnp.bfloat16
F32 = jnp.float32
AXES = ("node", "y", "z")
ORDER = ("z", "y", "node")
NT = (((1,), (1,)), ((), ()))
TN = (((0,), (0,)), ((), ()))


def dot(a, b, dims=(((1,), (0,)), ((), ()))):
    return lax.dot_general(a, b, dims, preferred_element_type=F32)


def over(a, n):
    assert n & (n - 1) == 0
    return lax.shift_right_logical(a, n.bit_length() - 1), a & (n - 1)


def row_tables(ids, first, rows, sizes):
    tokens = ids.shape[1]
    nodes, ys, pairs, halves = sizes
    device, row = over(first + lax.broadcasted_iota(jnp.int32, (rows, 1), 0), LOW)
    unit, node = over(device, nodes)
    z, y = over(unit, ys)
    expert = (node * ys + y) * pairs + over(z, halves)[0]
    hit = jnp.zeros((rows, tokens), F32)
    for k in range(ids.shape[0]):
        hit = hit + jnp.where(ids[k : k + 1, :] == expert, 1.0, 0.0)
    before = lax.broadcasted_iota(jnp.int32, (tokens, tokens), 0) < lax.broadcasted_iota(
        jnp.int32, (tokens, tokens), 1
    )
    rank = dot(hit.astype(BF), jnp.where(before, 1.0, 0.0).astype(BF)).astype(jnp.int32)
    return expert, row, hit, rank


def pack_kernel(sizes, ids_ref, gates_ref, x_ref, dy_ref, out_ref):
    nodes, ys, pairs, halves = sizes
    width = x_ref.shape[1]
    run = ys * nodes * LOW
    rows = out_ref.shape[0] // halves
    ids = ids_ref[...]
    gates = gates_ref[...].astype(F32)
    expert, row, hit, rank = row_tables(ids, pl.program_id(0) * rows, rows, (nodes, ys, pairs, 1))
    gate = jnp.zeros(hit.shape, F32)
    for k in range(ids.shape[0]):
        gate = gate + jnp.where(ids[k : k + 1, :] == expert, gates[k : k + 1, :], 0.0)
    low = jnp.where(rank == row, hit, 0.0)
    x, dy = x_ref[...], dy_ref[...]
    last = jnp.where(rank == LOW, hit, 0.0)
    piece = 2 * width // LOW
    masks, pieces = [], []
    for i in range(LOW):
        at = i * piece
        source, weight = (x, last) if at < width else (dy, last * gate)
        masks.append(jnp.where(row == i, weight, 0.0).astype(BF))
        pieces.append(source[:, at % width : at % width + piece])

    def put(value, to):
        value = value.astype(BF)
        for i in range(rows // run):
            for half in range(halves):
                first = (i * halves + half) * run
                out_ref[first : first + run, to] = value[i * run : (i + 1) * run]

    put(dot(low.astype(BF), x), slice(0, width))
    put(dot((low * gate).astype(BF), dy), slice(width, 2 * width))
    nine = dot(jnp.concatenate(masks, 1), jnp.concatenate(pieces, 0))
    put(nine, slice(2 * width, 2 * width + piece))


def piece_table(sources):
    shape = (sources * LOW, sources * LOW)
    a = lax.broadcasted_iota(jnp.int32, shape, 0)
    b = lax.broadcasted_iota(jnp.int32, shape, 1)
    piece, source = over(a, sources)
    return jnp.where(source * LOW + piece == b, 1.0, 0.0).astype(BF)


def nine_rows(got_ref, at, rows9):
    block = 32
    table = piece_table(block)
    x9, dy9 = [], []
    for first in range(0, rows9, block):
        pieces = dot(table, got_ref[first * LOW : (first + block) * LOW, at:]).astype(BF)
        pieces = [pieces[i * block : (i + 1) * block] for i in range(LOW)]
        x9.append(jnp.concatenate(pieces[: LOW // 2], 1))
        dy9.append(jnp.concatenate(pieces[LOW // 2 :], 1))
    return jnp.concatenate(x9, 0), jnp.concatenate(dy9, 0)


def unit_kernel(
    got_ref, gate_ref, up_ref, down_ref,
    back_hbm, dg_hbm, du_hbm, act_hbm, dg9_ref, du9_ref, act9_ref, x9_ref, dy9_ref,
    back_ref, dg_ref, du_ref, act_ref, done,
):
    width = gate_ref.shape[1]
    blocks, _, rows = dg_ref.shape
    sources = x9_ref.shape[0]
    piece = width // LOW
    tail = width + piece
    copies = []

    def send(source, target):
        copy = pltpu.make_async_copy(source, target, done.at[len(copies)])
        copy.start()
        copies.append(copy)

    def activations(x, dy):
        pre_gate = dot(gate_ref[...], x, NT)
        pre_up = dot(up_ref[...], x, NT)
        back = dot(down_ref[...], dy, NT)
        sig = jax.nn.sigmoid(pre_gate)
        silu = pre_gate * sig
        act = silu * pre_up
        part = jnp.sum(act * back, axis=0, keepdims=True)
        d_gate = (back * pre_up * (sig + silu * (1.0 - sig))).astype(BF)
        d_up = (back * silu).astype(BF)
        part = jnp.transpose(jnp.broadcast_to(part, (128, part.shape[1])))
        return d_gate, d_up, act.astype(BF), part

    def terms(d_gate, d_up):
        return (dot(d_gate, gate_ref[...], TN) + dot(d_up, up_ref[...], TN)).astype(BF)

    def start_block(i):
        at = slice(i * rows, (i + 1) * rows)
        d_gate, d_up, act, part = activations(got_ref[at, :width], got_ref[at, width : 2 * width])
        for held, out, value in (
            (dg_ref, dg_hbm, d_gate), (du_ref, du_hbm, d_up), (act_ref, act_hbm, act),
        ):
            held[i] = value
            send(held.at[i], out.at[:, pl.ds(i * rows, rows)])
        lane = lax.broadcasted_iota(jnp.int32, (rows, 128), 1)
        back_ref[at, tail:] = jnp.where(lane == 0, part, 0.0).astype(BF)
        return d_gate, d_up

    def end_block(i, d_gate, d_up):
        back_ref[i * rows : (i + 1) * rows, :width] = terms(d_gate, d_up)
        here = (pl.ds(i * rows, rows), pl.ds(0, width))
        send(back_ref.at[here], back_hbm.at[here])

    last = start_block(0)
    for i in range(1, blocks):
        now = start_block(i)
        end_block(i - 1, *last)
        last = now

    x9, dy9 = nine_rows(got_ref, 2 * width, sources)
    x9_ref[...], dy9_ref[...] = x9, dy9
    d_gate, d_up, act, part = activations(x9, dy9)
    dg9_ref[...], du9_ref[...], act9_ref[...] = d_gate, d_up, act
    end_block(blocks - 1, *last)
    term = terms(d_gate, d_up)
    block = 32
    table = piece_table(block)
    lane = lax.broadcasted_iota(jnp.int32, (block, 128), 1)
    for first in range(0, sources, block):
        at = slice(first, first + block)
        to = slice(first * LOW, (first + block) * LOW)
        pieces = [term[at, i * piece : (i + 1) * piece] for i in range(LOW)]
        back_ref[to, width:tail] = dot(table, jnp.concatenate(pieces, 0), TN).astype(BF)
        part9 = jnp.where(lane == 1, part[at], 0.0).astype(BF)
        part9 = dot(table[:block], part9, TN)
        back_ref[to, tail:] = (back_ref[to, tail:].astype(F32) + part9).astype(BF)
    here = (slice(None), pl.ds(width, piece + 128))
    send(back_ref.at[here], back_hbm.at[here])
    for copy in copies:
        copy.wait()


def collect_kernel(sizes, ids_ref, gates_ref, back_ref, out_ref, gg_ref, sum_ref, part_ref):
    rows, width = back_ref.shape[0], out_ref.shape[1]
    step = pl.program_id(0)
    ids = ids_ref[...]
    top, count = ids.shape
    first = step * rows
    expert, row, hit, rank = row_tables(ids, first, rows, sizes)
    low = jnp.where(rank == row, hit, 0.0)
    last = jnp.where(rank == LOW, hit, 0.0)
    piece = width // LOW

    @pl.when(step == 0)
    def _():
        sum_ref[...] = jnp.zeros_like(sum_ref)
        part_ref[...] = jnp.zeros_like(part_ref)

    low_t, last_t = jnp.transpose(low), jnp.transpose(last)
    row_t = over(lax.broadcasted_iota(jnp.int32, (1, rows), 1), LOW)[1]
    masks = jnp.concatenate(
        [jnp.where(row_t == i, last_t, 0.0).astype(BF) for i in range(LOW)], 0
    )
    pieces = dot(masks, back_ref[:, width : width + piece])
    total = dot(low_t.astype(BF), back_ref[:, :width])
    for i in range(LOW):
        at = slice(i * piece, (i + 1) * piece)
        sum_ref[:, at] += total[:, at] + pieces[i * count : (i + 1) * count]
    parts = back_ref[:, width + piece :].astype(F32)
    mine = low * parts[:, 0:1] + jnp.where(row == 0, last, 0.0) * parts[:, 1:2]
    for k in range(top):
        part_ref[k : k + 1, :] += jnp.sum(
            jnp.where(ids[k : k + 1, :] == expert, mine, 0.0), axis=0, keepdims=True
        )

    @pl.when(step == pl.num_programs(0) - 1)
    def _():
        out_ref[...] = sum_ref[...].astype(BF)
        gg_ref[...] = part_ref[:top, :] / gates_ref[...].astype(F32)


def whole(shape):
    return pl.BlockSpec(shape, lambda b: (0,) * len(shape))


def split(shape):
    return pl.BlockSpec(shape, lambda b: (b,) + (0,) * (len(shape) - 1))


def limits(mib):
    return pltpu.CompilerParams(
        dimension_semantics=("arbitrary",), vmem_limit_bytes=mib * 2**20
    )


def local(tokens, cotangent, gate_weights, expert_ids, gate_proj, up_proj, down_proj):
    nodes, ys, zs = (lax.axis_size(name) for name in AXES)
    devices = nodes * ys * zs
    count, width = tokens.shape
    hidden = down_proj.shape[1]
    halves = 2
    sizes = (nodes, ys, zs // halves, halves)
    slots = devices * LOW
    top = expert_ids.shape[1]
    ids_t, gates_t = jnp.swapaxes(expert_ids, 0, 1), jnp.swapaxes(gate_weights, 0, 1)

    blocks = zs // halves
    message = 2 * width + 2 * width // LOW
    sent = pl.pallas_call(
        lambda *refs: pack_kernel(sizes, *refs),
        grid=(blocks,),
        in_specs=[
            whole((top, count)), whole((top, count)), whole((count, width)), whole((count, width)),
        ],
        out_specs=split((slots // blocks, message)),
        out_shape=jax.ShapeDtypeStruct((slots, message), BF),
        compiler_params=limits(60),
        name="pack_rows",
    )(ids_t, gates_t, tokens, cotangent)

    got = lax.all_to_all(
        sent.reshape(devices, LOW, message), ORDER, split_axis=0, concat_axis=0, tiled=True
    ).reshape(slots, message)

    gate_t = jnp.swapaxes(gate_proj[0], 0, 1)
    up_t = jnp.swapaxes(up_proj[0], 0, 1)
    down = down_proj[0]
    blocks = 4
    rows = slots // blocks
    piece = width // LOW
    reply = width + piece + 128
    gate_t, up_t, down, held = (
        pltpu.with_memory_space_constraint(w, pltpu.VMEM) for w in (gate_t, up_t, down, got)
    )
    inside = pl.BlockSpec(memory_space=pltpu.VMEM)
    outside = pl.BlockSpec(memory_space=pl.ANY)
    term, d_gate, d_up, act, d_gate9, d_up9, act9, x9, dy9 = pl.pallas_call(
        unit_kernel,
        in_specs=[inside] * 4,
        out_specs=[outside] * 4 + [inside] * 5,
        out_shape=[jax.ShapeDtypeStruct((slots, reply), BF)]
        + [jax.ShapeDtypeStruct((hidden, slots), BF)] * 3
        + [jax.ShapeDtypeStruct((hidden, devices), BF)] * 3
        + [jax.ShapeDtypeStruct((devices, width), BF)] * 2,
        scratch_shapes=[pltpu.VMEM((slots, reply), BF)]
        + [pltpu.VMEM((blocks, hidden, rows), BF)] * 3
        + [pltpu.SemaphoreType.DMA((4 * blocks + 1,))],
        compiler_params=pltpu.CompilerParams(vmem_limit_bytes=40 * 2**20),
        name="unit_terms",
    )(held, gate_t, up_t, down)

    returned = lax.all_to_all(
        term.reshape(devices, LOW, reply), ORDER, split_axis=0, concat_axis=0, tiled=True
    ).reshape(slots, reply)

    x8, dy8 = got[:, :width], got[:, width : 2 * width]
    grad_gate = (dot(d_gate, x8) + dot(d_gate9, x9)).astype(BF)
    grad_up = (dot(d_up, x8) + dot(d_up9, x9)).astype(BF)
    grad_gate, grad_up = jnp.swapaxes(grad_gate, 0, 1), jnp.swapaxes(grad_up, 0, 1)
    grad_down = (dot(act, dy8) + dot(act9, dy9)).astype(BF)

    blocks = 2
    grad_tokens, grad_gates = pl.pallas_call(
        lambda *refs: collect_kernel(sizes, *refs),
        grid=(blocks,),
        in_specs=[whole((top, count)), whole((top, count)), split((slots // blocks, reply))],
        out_specs=[whole((count, width)), whole((top, count))],
        out_shape=[
            jax.ShapeDtypeStruct((count, width), BF),
            jax.ShapeDtypeStruct((top, count), F32),
        ],
        scratch_shapes=[pltpu.VMEM((count, width), F32), pltpu.VMEM((8, count), F32)],
        compiler_params=limits(48),
        name="collect_rows",
    )(ids_t, gates_t, returned)
    grad_gates = jnp.swapaxes(grad_gates, 0, 1)
    return grad_tokens, grad_gates, grad_gate[None], grad_up[None], grad_down[None]


def solution(mesh):
    nodes, members = mesh.devices.shape
    side = math.isqrt(members)
    mesh = jax.sharding.Mesh(mesh.devices.reshape(nodes, side, members // side), AXES)
    row = P(AXES, None)
    unit = P(AXES, None, None)
    return jax.shard_map(
        local,
        mesh=mesh,
        in_specs=(row, row, row, row, unit, unit, unit),
        out_specs=(row, row, unit, unit, unit),
        check_vma=False,
    )
```

```python
import math

import jax
import jax.numpy as jnp
from jax import lax
from jax.experimental import pallas as pl
from jax.experimental.pallas import tpu as pltpu
from jax.sharding import PartitionSpec as P

LOW = 8
BF = jnp.bfloat16
F32 = jnp.float32
AXES = ("node", "y", "z")
ORDER = ("z", "y", "node")
NT = (((1,), (1,)), ((), ()))
TN = (((0,), (0,)), ((), ()))


def dot(a, b, dims=(((1,), (0,)), ((), ()))):
    return lax.dot_general(a, b, dims, preferred_element_type=F32)


def over(a, n):
    assert n & (n - 1) == 0
    return lax.shift_right_logical(a, n.bit_length() - 1), a & (n - 1)


def row_tables(ids, first, rows, sizes):
    tokens = ids.shape[1]
    nodes, ys, pairs, halves = sizes
    device, row = over(first + lax.broadcasted_iota(jnp.int32, (rows, 1), 0), LOW)
    unit, node = over(device, nodes)
    z, y = over(unit, ys)
    expert = (node * ys + y) * pairs + over(z, halves)[0]
    hit = jnp.zeros((rows, tokens), F32)
    for k in range(ids.shape[0]):
        hit = hit + jnp.where(ids[k : k + 1, :] == expert, 1.0, 0.0)
    before = lax.broadcasted_iota(jnp.int32, (tokens, tokens), 0) < lax.broadcasted_iota(
        jnp.int32, (tokens, tokens), 1
    )
    rank = dot(hit.astype(BF), jnp.where(before, 1.0, 0.0).astype(BF)).astype(jnp.int32)
    return expert, row, hit, rank


def pack_kernel(sizes, ids_ref, gates_ref, x_ref, dy_ref, out_ref):
    nodes, ys, pairs, halves = sizes
    width = x_ref.shape[1]
    run = ys * nodes * LOW
    rows = out_ref.shape[0] // halves
    ids = ids_ref[...]
    gates = gates_ref[...].astype(F32)
    expert, row, hit, rank = row_tables(ids, pl.program_id(0) * rows, rows, (nodes, ys, pairs, 1))
    gate = jnp.zeros(hit.shape, F32)
    for k in range(ids.shape[0]):
        gate = gate + jnp.where(ids[k : k + 1, :] == expert, gates[k : k + 1, :], 0.0)
    low = jnp.where(rank == row, hit, 0.0)
    x, dy = x_ref[...], dy_ref[...]
    last = jnp.where(rank == LOW, hit, 0.0)
    piece = 2 * width // LOW
    masks, pieces = [], []
    for i in range(LOW):
        at = i * piece
        source, weight = (x, last) if at < width else (dy, last * gate)
        masks.append(jnp.where(row == i, weight, 0.0).astype(BF))
        pieces.append(source[:, at % width : at % width + piece])

    def put(value, to):
        value = value.astype(BF)
        for i in range(rows // run):
            for half in range(halves):
                first = (i * halves + half) * run
                out_ref[first : first + run, to] = value[i * run : (i + 1) * run]

    put(dot(low.astype(BF), x), slice(0, width))
    put(dot((low * gate).astype(BF), dy), slice(width, 2 * width))
    nine = dot(jnp.concatenate(masks, 1), jnp.concatenate(pieces, 0))
    put(nine, slice(2 * width, 2 * width + piece))


def piece_table(sources):
    shape = (sources * LOW, sources * LOW)
    a = lax.broadcasted_iota(jnp.int32, shape, 0)
    b = lax.broadcasted_iota(jnp.int32, shape, 1)
    piece, source = over(a, sources)
    return jnp.where(source * LOW + piece == b, 1.0, 0.0).astype(BF)


def nine_rows(got_ref, at, rows9):
    block = 32
    table = piece_table(block)
    x9, dy9 = [], []
    for first in range(0, rows9, block):
        pieces = dot(table, got_ref[first * LOW : (first + block) * LOW, at:]).astype(BF)
        pieces = [pieces[i * block : (i + 1) * block] for i in range(LOW)]
        x9.append(jnp.concatenate(pieces[: LOW // 2], 1))
        dy9.append(jnp.concatenate(pieces[LOW // 2 :], 1))
    return jnp.concatenate(x9, 0), jnp.concatenate(dy9, 0)


def unit_kernel(
    got_ref, gate_ref, up_ref, down_ref,
    back_hbm, dg_hbm, du_hbm, act_hbm, dg9_ref, du9_ref, act9_ref, x9_ref, dy9_ref,
    back_ref, dg_ref, du_ref, act_ref, done,
):
    width = gate_ref.shape[1]
    blocks, _, rows = dg_ref.shape
    sources = x9_ref.shape[0]
    piece = width // LOW
    tail = width + piece
    copies = []

    def send(source, target):
        copy = pltpu.make_async_copy(source, target, done.at[len(copies)])
        copy.start()
        copies.append(copy)

    def activations(x, dy):
        pre_gate = dot(gate_ref[...], x, NT)
        pre_up = dot(up_ref[...], x, NT)
        back = dot(down_ref[...], dy, NT)
        sig = jax.nn.sigmoid(pre_gate)
        silu = pre_gate * sig
        act = silu * pre_up
        part = jnp.sum(act * back, axis=0, keepdims=True)
        d_gate = (back * pre_up * (sig + silu * (1.0 - sig))).astype(BF)
        d_up = (back * silu).astype(BF)
        part = jnp.transpose(jnp.broadcast_to(part, (128, part.shape[1])))
        return d_gate, d_up, act.astype(BF), part

    def terms(d_gate, d_up):
        return (dot(d_gate, gate_ref[...], TN) + dot(d_up, up_ref[...], TN)).astype(BF)

    def start_block(i):
        at = slice(i * rows, (i + 1) * rows)
        d_gate, d_up, act, part = activations(got_ref[at, :width], got_ref[at, width : 2 * width])
        for held, out, value in (
            (dg_ref, dg_hbm, d_gate), (du_ref, du_hbm, d_up), (act_ref, act_hbm, act),
        ):
            held[i] = value
            send(held.at[i], out.at[:, pl.ds(i * rows, rows)])
        lane = lax.broadcasted_iota(jnp.int32, (rows, 128), 1)
        back_ref[at, tail:] = jnp.where(lane == 0, part, 0.0).astype(BF)
        return d_gate, d_up

    def end_block(i, d_gate, d_up):
        back_ref[i * rows : (i + 1) * rows, :width] = terms(d_gate, d_up)
        here = (pl.ds(i * rows, rows), pl.ds(0, width))
        send(back_ref.at[here], back_hbm.at[here])

    last = start_block(0)
    for i in range(1, blocks - 1):
        now = start_block(i)
        end_block(i - 1, *last)
        last = now

    x9, dy9 = nine_rows(got_ref, 2 * width, sources)
    x9_ref[...], dy9_ref[...] = x9, dy9
    d_gate, d_up, act, part = activations(x9, dy9)
    dg9_ref[...], du9_ref[...], act9_ref[...] = d_gate, d_up, act
    end_block(blocks - 2, *last)
    last = start_block(blocks - 1)
    term = terms(d_gate, d_up)
    block = 32
    table = piece_table(block)
    lane = lax.broadcasted_iota(jnp.int32, (block, 128), 1)
    for first in range(0, sources, block):
        at = slice(first, first + block)
        to = slice(first * LOW, (first + block) * LOW)
        pieces = [term[at, i * piece : (i + 1) * piece] for i in range(LOW)]
        back_ref[to, width:tail] = dot(table, jnp.concatenate(pieces, 0), TN).astype(BF)
        part9 = jnp.where(lane == 1, part[at], 0.0).astype(BF)
        part9 = dot(table[:block], part9, TN)
        back_ref[to, tail:] = (back_ref[to, tail:].astype(F32) + part9).astype(BF)
    here = (slice(None), pl.ds(width, piece + 128))
    send(back_ref.at[here], back_hbm.at[here])
    end_block(blocks - 1, *last)
    for copy in copies:
        copy.wait()


def collect_kernel(sizes, ids_ref, gates_ref, back_ref, out_ref, gg_ref, sum_ref, part_ref):
    rows, width = back_ref.shape[0], out_ref.shape[1]
    step = pl.program_id(0)
    ids = ids_ref[...]
    top, count = ids.shape
    first = step * rows
    expert, row, hit, rank = row_tables(ids, first, rows, sizes)
    low = jnp.where(rank == row, hit, 0.0)
    last = jnp.where(rank == LOW, hit, 0.0)
    piece = width // LOW

    @pl.when(step == 0)
    def _():
        sum_ref[...] = jnp.zeros_like(sum_ref)
        part_ref[...] = jnp.zeros_like(part_ref)

    low_t, last_t = jnp.transpose(low), jnp.transpose(last)
    row_t = over(lax.broadcasted_iota(jnp.int32, (1, rows), 1), LOW)[1]
    masks = jnp.concatenate(
        [jnp.where(row_t == i, last_t, 0.0).astype(BF) for i in range(LOW)], 0
    )
    pieces = dot(masks, back_ref[:, width : width + piece])
    total = dot(low_t.astype(BF), back_ref[:, :width])
    for i in range(LOW):
        at = slice(i * piece, (i + 1) * piece)
        sum_ref[:, at] += total[:, at] + pieces[i * count : (i + 1) * count]
    parts = back_ref[:, width + piece :].astype(F32)
    mine = low * parts[:, 0:1] + jnp.where(row == 0, last, 0.0) * parts[:, 1:2]
    for k in range(top):
        part_ref[k : k + 1, :] += jnp.sum(
            jnp.where(ids[k : k + 1, :] == expert, mine, 0.0), axis=0, keepdims=True
        )

    @pl.when(step == pl.num_programs(0) - 1)
    def _():
        out_ref[...] = sum_ref[...].astype(BF)
        gg_ref[...] = part_ref[:top, :] / gates_ref[...].astype(F32)


def whole(shape):
    return pl.BlockSpec(shape, lambda b: (0,) * len(shape))


def split(shape):
    return pl.BlockSpec(shape, lambda b: (b,) + (0,) * (len(shape) - 1))


def limits(mib):
    return pltpu.CompilerParams(
        dimension_semantics=("arbitrary",), vmem_limit_bytes=mib * 2**20
    )


def local(tokens, cotangent, gate_weights, expert_ids, gate_proj, up_proj, down_proj):
    nodes, ys, zs = (lax.axis_size(name) for name in AXES)
    devices = nodes * ys * zs
    count, width = tokens.shape
    hidden = down_proj.shape[1]
    halves = 2
    sizes = (nodes, ys, zs // halves, halves)
    slots = devices * LOW
    top = expert_ids.shape[1]
    ids_t, gates_t = jnp.swapaxes(expert_ids, 0, 1), jnp.swapaxes(gate_weights, 0, 1)

    blocks = zs // halves
    message = 2 * width + 2 * width // LOW
    sent = pl.pallas_call(
        lambda *refs: pack_kernel(sizes, *refs),
        grid=(blocks,),
        in_specs=[
            whole((top, count)), whole((top, count)), whole((count, width)), whole((count, width)),
        ],
        out_specs=split((slots // blocks, message)),
        out_shape=jax.ShapeDtypeStruct((slots, message), BF),
        compiler_params=limits(60),
        name="pack_rows",
    )(ids_t, gates_t, tokens, cotangent)

    got = lax.all_to_all(
        sent.reshape(devices, LOW, message), ORDER, split_axis=0, concat_axis=0, tiled=True
    ).reshape(slots, message)

    gate_t = jnp.swapaxes(gate_proj[0], 0, 1)
    up_t = jnp.swapaxes(up_proj[0], 0, 1)
    down = down_proj[0]
    blocks = 4
    rows = slots // blocks
    piece = width // LOW
    reply = width + piece + 128
    gate_t, up_t, down, held = (
        pltpu.with_memory_space_constraint(w, pltpu.VMEM) for w in (gate_t, up_t, down, got)
    )
    inside = pl.BlockSpec(memory_space=pltpu.VMEM)
    outside = pl.BlockSpec(memory_space=pl.ANY)
    term, d_gate, d_up, act, d_gate9, d_up9, act9, x9, dy9 = pl.pallas_call(
        unit_kernel,
        in_specs=[inside] * 4,
        out_specs=[outside] * 4 + [inside] * 5,
        out_shape=[jax.ShapeDtypeStruct((slots, reply), BF)]
        + [jax.ShapeDtypeStruct((hidden, slots), BF)] * 3
        + [jax.ShapeDtypeStruct((hidden, devices), BF)] * 3
        + [jax.ShapeDtypeStruct((devices, width), BF)] * 2,
        scratch_shapes=[pltpu.VMEM((slots, reply), BF)]
        + [pltpu.VMEM((blocks, hidden, rows), BF)] * 3
        + [pltpu.SemaphoreType.DMA((4 * blocks + 1,))],
        compiler_params=pltpu.CompilerParams(vmem_limit_bytes=40 * 2**20),
        name="unit_terms",
    )(held, gate_t, up_t, down)

    returned = lax.all_to_all(
        term.reshape(devices, LOW, reply), ORDER, split_axis=0, concat_axis=0, tiled=True
    ).reshape(slots, reply)

    x8, dy8 = got[:, :width], got[:, width : 2 * width]
    grad_gate = (dot(d_gate, x8) + dot(d_gate9, x9)).astype(BF)
    grad_up = (dot(d_up, x8) + dot(d_up9, x9)).astype(BF)
    grad_gate, grad_up = jnp.swapaxes(grad_gate, 0, 1), jnp.swapaxes(grad_up, 0, 1)
    grad_down = (dot(act, dy8) + dot(act9, dy9)).astype(BF)

    blocks = 2
    grad_tokens, grad_gates = pl.pallas_call(
        lambda *refs: collect_kernel(sizes, *refs),
        grid=(blocks,),
        in_specs=[whole((top, count)), whole((top, count)), split((slots // blocks, reply))],
        out_specs=[whole((count, width)), whole((top, count))],
        out_shape=[
            jax.ShapeDtypeStruct((count, width), BF),
            jax.ShapeDtypeStruct((top, count), F32),
        ],
        scratch_shapes=[pltpu.VMEM((count, width), F32), pltpu.VMEM((8, count), F32)],
        compiler_params=limits(48),
        name="collect_rows",
    )(ids_t, gates_t, returned)
    grad_gates = jnp.swapaxes(grad_gates, 0, 1)
    return grad_tokens, grad_gates, grad_gate[None], grad_up[None], grad_down[None]


def solution(mesh):
    nodes, members = mesh.devices.shape
    side = math.isqrt(members)
    mesh = jax.sharding.Mesh(mesh.devices.reshape(nodes, side, members // side), AXES)
    row = P(AXES, None)
    unit = P(AXES, None, None)
    return jax.shard_map(
        local,
        mesh=mesh,
        in_specs=(row, row, row, row, unit, unit, unit),
        out_specs=(row, row, unit, unit, unit),
        check_vma=False,
    )
```
